256 devices in a mesh: row: 8 (over x, z_lo), col: 32 (over z_hi, y, core).
Axes of the slice: x: 4, y: 4, z: 8 (z_hi: 4, z_lo: 2; z = z_hi * 2 + z_lo), core: 2. Of those that a mesh axis runs over, the one named last changes fastest.
Arguments:
- pair: float32 [512, 512, 128], P('row', 'col'), may hold values from -6 to 6
- pair_mask: int32 [512, 512], P('row', 'col'), may hold values from 0 to 1, as said below
- cotangent: float32 [512, 512, 128], P('row', 'col'), may hold values from -6 to 6
- in_gain: float32 [128], replicated, may hold values from 0.25 to 1.75
- in_bias: float32 [128], replicated, may hold values from -2 to 2
- left_weight: bfloat16 [128, 128], replicated, may hold values from -0.5 to 0.5
- left_gate_weight: bfloat16 [128, 128], replicated, may hold values from -0.5 to 0.5
- right_weight: bfloat16 [128, 128], replicated, may hold values from -0.5 to 0.5
- right_gate_weight: bfloat16 [128, 128], replicated, may hold values from -0.5 to 0.5
- out_gain: float32 [128], replicated, may hold values from 0.25 to 1.75
- out_bias: float32 [128], replicated, may hold values from -2 to 2
- output_weight: bfloat16 [128, 128], replicated, may hold values from -0.5 to 0.5
- output_gate_weight: bfloat16 [128, 128], replicated, may hold values from -0.5 to 0.5
Outputs:
- update: float32 [512, 512, 128], P('row', 'col')
- grad_pair: float32 [512, 512, 128], P('row', 'col')
- grad_left: float32 [128, 128], replicated
- grad_left_gate: float32 [128, 128], replicated
- grad_right: float32 [128, 128], replicated
- grad_right_gate: float32 [128, 128], replicated
- grad_output: float32 [128, 128], replicated
- grad_output_gate: float32 [128, 128], replicated
- grad_norms: float32 [4, 128], replicated
The draws below stay inside these ranges and needn't reach their ends.
Inputs may be any that keep to these rules, and one draw needn't show every extreme that they name: `pair_mask`: pair_mask_ij = r_i * r_j for a 0/1 residue mask r of 512 entries; r holds at least one 0 and at least one 1.
All inputs are finite; a program needn't handle non-finite values.
Results may differ from the reference program's by a relative error of at most 0.0067.
Values may be sent and summed in bfloat16 or wider, within the bound.
A program may use at most 128 MiB of HBM per device.

```python
import jax
import jax.numpy as jnp
from jax import lax

C = 128
H = 128
N = 512


def draw_pair_mask(key, part):
    key = jax.random.fold_in(key, 7)
    key_bits, key_zero, key_one = jax.random.split(key, 3)
    positions = jnp.arange(N)
    valid = jax.random.randint(key_bits, (N,), 0, 100) < 85
    zero_at = jax.random.randint(key_zero, (), 0, N)
    one_at = (zero_at + 1 + jax.random.randint(key_one, (), 0, N - 1)) % N
    valid = valid & (positions != zero_at) | (positions == one_at)
    return (valid[:, None] & valid[None, :]).astype(jnp.int32)


def block_levels(own_key, shape, pieces, low, high):
    level, own = 1.0, jax.random.fold_in(own_key, 6)
    for position, parts in pieces:
        draws = jnp.exp(jax.random.uniform(jax.random.fold_in(own, position), (parts,), jnp.float32, low / len(pieces), high / len(pieces)))
        level = level * jnp.repeat(draws, shape[position] // parts).reshape([-1 if axis == position else 1 for axis in range(len(shape))])
    return level


def gaussian(key, shape, deviation, reach, cuts=(), kind=jnp.bfloat16):
    drawn = deviation * jax.random.normal(key, shape, jnp.float32)
    if cuts:
        drawn = drawn * block_levels(key, shape, cuts, -0.22, 0.18)
    return jnp.clip(drawn, -reach, reach).astype(kind)


def setup_inputs(seed: int = 0) -> dict:
    streams_of = jax.random.split(jax.random.key(seed), 14)
    return {
        "pair": gaussian(streams_of[0], (N, N, C), 1.0, 6.0, ((0, 8), (1, 32)), jnp.float32),
        "pair_mask": draw_pair_mask(jax.random.fold_in(streams_of[13], 71), 0),
        "cotangent": gaussian(streams_of[2], (N, N, C), 1.0, 6.0, ((0, 8), (1, 32)), jnp.float32),
        "in_gain": jnp.clip(1.0 + 0.15 * jax.random.normal(streams_of[3], (C,), jnp.float32), 0.25, 1.75),
        "in_bias": gaussian(streams_of[4], (C,), 0.3, 2.0, (), jnp.float32),
        "left_weight": gaussian(streams_of[5], (C, H), C ** -0.5, 0.5),
        "left_gate_weight": gaussian(streams_of[6], (C, H), C ** -0.5, 0.5),
        "right_weight": gaussian(streams_of[7], (C, H), C ** -0.5, 0.5),
        "right_gate_weight": gaussian(streams_of[8], (C, H), C ** -0.5, 0.5),
        "out_gain": jnp.clip(1.0 + 0.15 * jax.random.normal(streams_of[9], (H,), jnp.float32), 0.25, 1.75),
        "out_bias": gaussian(streams_of[10], (H,), 0.3, 2.0, (), jnp.float32),
        "output_weight": gaussian(streams_of[11], (H, C), H ** -0.5, 0.5),
        "output_gate_weight": gaussian(streams_of[12], (C, C), C ** -0.5, 0.5),
    }


EPS = 1e-05

def norm_forward(value, gain, bias):
    center = value - lax.optimization_barrier(jnp.mean(value, axis=-1, keepdims=True))
    rstd = lax.rsqrt(lax.optimization_barrier(jnp.mean(center * center, axis=-1, keepdims=True)) + EPS)
    hat = center * rstd
    return (hat * gain + bias, hat, rstd)

def norm_backward(grad_out, hat, rstd, gain):
    dhat = grad_out * gain
    return rstd * (dhat - lax.optimization_barrier(jnp.mean(dhat, axis=-1, keepdims=True)) - hat * lax.optimization_barrier(jnp.mean(dhat * hat, axis=-1, keepdims=True)))

def matmul(left_in, weight):
    return jnp.dot(left_in, weight, preferred_element_type=jnp.float32)

def outer_sum(first, second):
    return jnp.einsum('ijc,ijh->ch', first.astype(jnp.float32), second.astype(jnp.float32))

def reference(pair, pair_mask, cotangent, in_gain, in_bias, left_weight, left_gate_weight, right_weight, right_gate_weight, out_gain, out_bias, output_weight, output_gate_weight):
    normed_f, in_hat, in_rstd = norm_forward(pair, in_gain, in_bias)
    normed = normed_f.astype(jnp.bfloat16)
    maskf = pair_mask.astype(jnp.float32)[..., None]
    left_v = matmul(normed, left_weight)
    left_s = jax.nn.sigmoid(matmul(normed, left_gate_weight))
    right_v = matmul(normed, right_weight)
    right_s = jax.nn.sigmoid(matmul(normed, right_gate_weight))
    left = (left_s * left_v * maskf).astype(jnp.bfloat16)
    right = (right_s * right_v * maskf).astype(jnp.bfloat16)
    tri = jnp.einsum('ikh,jkh->ijh', left.astype(jnp.float32), right.astype(jnp.float32))
    tri_f, tri_hat, tri_rstd = norm_forward(tri, out_gain, out_bias)
    tri_normed = tri_f.astype(jnp.bfloat16)
    gate = jax.nn.sigmoid(matmul(normed, output_gate_weight))
    proj = matmul(tri_normed, output_weight)
    update = gate * proj
    d_out = (cotangent * gate).astype(jnp.bfloat16)
    d_gate = (cotangent * proj * gate * (1.0 - gate)).astype(jnp.bfloat16)
    d_tri_normed = matmul(d_out, output_weight.T)
    d_tri = norm_backward(d_tri_normed, tri_hat, tri_rstd, out_gain).astype(jnp.bfloat16)
    d_left = jnp.einsum('ijh,jkh->ikh', d_tri.astype(jnp.float32), right.astype(jnp.float32))
    d_right = jnp.einsum('ijh,ikh->jkh', d_tri.astype(jnp.float32), left.astype(jnp.float32))
    dv_left = (d_left * left_s * maskf).astype(jnp.bfloat16)
    du_left = (d_left * left_v * maskf * left_s * (1.0 - left_s)).astype(jnp.bfloat16)
    dv_right = (d_right * right_s * maskf).astype(jnp.bfloat16)
    du_right = (d_right * right_v * maskf * right_s * (1.0 - right_s)).astype(jnp.bfloat16)
    d_normed = matmul(dv_left, left_weight.T) + matmul(du_left, left_gate_weight.T) + matmul(dv_right, right_weight.T) + matmul(du_right, right_gate_weight.T) + matmul(d_gate, output_gate_weight.T)
    grad_pair = norm_backward(d_normed, in_hat, in_rstd, in_gain)
    scale = 1.0 / N
    grad_norms = jnp.stack([lax.optimization_barrier(jnp.sum(d_normed * in_hat, axis=(0, 1))), lax.optimization_barrier(jnp.sum(d_normed, axis=(0, 1))), lax.optimization_barrier(jnp.sum(d_tri_normed * tri_hat, axis=(0, 1))), lax.optimization_barrier(jnp.sum(d_tri_normed, axis=(0, 1)))])
    return (update, grad_pair, outer_sum(normed, dv_left) * scale, outer_sum(normed, du_left) * scale, outer_sum(normed, dv_right) * scale, outer_sum(normed, du_right) * scale, outer_sum(tri_normed, d_out) * scale, outer_sum(normed, d_gate) * scale, grad_norms * scale)
```

```python
import functools

import jax
import jax.numpy as jnp
from jax import lax
from jax.experimental import pallas as pl
from jax.experimental.pallas import tpu as pltpu
from jax.sharding import PartitionSpec as P

EPS = 1e-05
MESH = pl.DeviceIdType.MESH
F32, BF16 = jnp.float32, jnp.bfloat16
X1, P1, P2, X2, P3, X3, P4, X4, A1, A2, A3, A4, A5 = range(13)


def dot(a, b, ca, cb):
    return lax.dot_general(a, b, (((ca,), (cb,)), ((), ())), preferred_element_type=F32)


def swap_halves(a, b):
    low = lax.broadcasted_iota(jnp.int32, a.shape, 1) < 64
    return jnp.where(low, a, pltpu.roll(b, 64, 1)), jnp.where(low, pltpu.roll(a, 64, 1), b)


def kernel(
    pair, cot, mask, in_gain, in_bias, wl, wlg, wr, wrg, out_gain, out_bias, wo, wog,
    update, grad_pair, g_left, g_left_gate, g_right, g_right_gate, g_out, g_out_gate, g_norms,
    xin, cin, wcat, wcat_t, hat_in, rstd_in, normed, vs, stage, gate, slope, d_out, d_tn, tri_n, tri_f, d_gate, dn, dx,
    cols, acc, give1, send1, got1, lk, rk, tt, send2, got2, give2, take2, give3, take3, send3, got3, dt, ol, orr,
    send4, got4, take4, part, a1_give, a1_take, a2_send, a2_got, a3_send, a3_got, a4_send, a4_got, a5_take,
    in_sems, ssem, rsem, ready,
):
    row, col = lax.axis_index("row"), lax.axis_index("col")
    cc, q = col // 2, col % 2
    x, zl, zh, y = row // 2, row % 2, cc // 4, cc % 4
    z = zh * 2 + zl
    me = row * 16 + cc
    own = row // 4 == q
    not_own = jnp.logical_not(own)
    chan = (row % 4) * 16 + cc
    plane = x * 4 + y
    sibling = (row, cc * 2 + 1 - q)

    def remote(src, dst, k, dev):
        return pltpu.make_async_remote_copy(
            src_ref=src, dst_ref=dst, send_sem=ssem.at[k], recv_sem=rsem.at[k], device_id=dev, device_id_type=MESH
        )

    def wait_slots(buf, n, sem):
        pltpu.make_async_copy(buf.at[pl.ds(0, n)], buf.at[pl.ds(0, n)], sem).wait()

    def each_owner(fn):
        rows = [q * 4 + (row + d) % 4 for d in range(4)]

        @pl.when(not_own)
        def _():
            fn((rows[0], col), rows[0] % 4 * 16 + cc)

        for d in range(1, 4):
            fn((rows[d], col), rows[d] % 4 * 16 + cc)

        def step(e, carry):
            c = (cc + e) % 16
            for d in range(4):
                fn((rows[d], c * 2 + q), rows[d] % 4 * 16 + c)
            return carry

        lax.fori_loop(1, 16, step, 0)

    def each_chip(fn):
        rows = [(row + d) % 8 for d in range(8)]
        for d in range(1, 8):
            fn((rows[d], col), rows[d] * 16 + cc)

        def step(e, carry):
            c = (cc + e) % 16
            for d in range(8):
                fn((rows[d], c * 2 + q), rows[d] * 16 + c)
            return carry

        lax.fori_loop(1, 16, step, 0)

    def each_plane(fn):
        def step(d, carry):
            px, py = (x + d // 4) % 4, (y + d) % 4
            fn((px * 2 + zl, (zh * 4 + py) * 2 + q), px * 4 + py)
            return carry

        lax.fori_loop(1, 16, step, 0)

    def each_z(fn):
        def step(d, carry):
            pz = (z + d) % 8
            fn((x * 2 + pz % 2, (pz // 2 * 4 + y) * 2 + q), pz)
            return carry

        lax.fori_loop(1, 8, step, 0)

    def wait_owners(buf, sem):
        @pl.when(own)
        def _():
            wait_slots(buf, 63, sem)

        @pl.when(not_own)
        def _():
            wait_slots(buf, 64, sem)

    def signal(sem, dev):
        pl.semaphore_signal(sem, inc=1, device_id=dev, device_id_type=MESH)

    def cells(ref, s, put=None):
        for h in range(4):
            p, par = h // 2, h % 2
            at = pl.ds(par * 16 + 2 * s + p, 32, stride=32)
            if put is not None:
                ref[at, :] = put[h * 32 : h * 32 + 32]
        if put is None:
            return jnp.concatenate(
                [ref[pl.ds(par * 16 + 2 * s + p, 32, stride=32), :] for p in range(2) for par in range(2)], axis=0
            )

    load_pair = pltpu.make_async_copy(pair, xin, in_sems.at[0])
    load_cot = pltpu.make_async_copy(cot, cin, in_sems.at[1])
    load_pair.start()
    load_cot.start()
    bar = pltpu.get_barrier_semaphore()
    signal(bar, sibling)
    each_z(lambda dev, i: signal(bar, dev))
    each_plane(lambda dev, i: signal(bar, dev))

    wcat[...] = jnp.concatenate([wl[...], wlg[...], wr[...], wrg[...]], axis=1)
    for i, w in enumerate((wl, wlg, wr, wrg)):
        wcat_t[i * 128 : i * 128 + 128, :] = w[...].astype(F32).T.astype(BF16)
    cols[0] = jnp.broadcast_to(out_gain[...], (128, 128)).T
    cols[1] = jnp.broadcast_to(out_bias[...], (128, 128)).T
    load_pair.wait()

    def project(s, carry):
        v = cells(xin, s)
        center = v - jnp.mean(v, axis=-1, keepdims=True)
        rstd = lax.rsqrt(jnp.mean(center * center, axis=-1, keepdims=True) + EPS)
        hat = center * rstd
        n = (hat * in_gain[...] + in_bias[...]).astype(BF16)
        hat_in[s] = hat
        rstd_in[s] = rstd
        normed[s] = n
        both = dot(wcat_t[...], n, 1, 1)
        m = mask[pl.ds(s, 1), :]
        for side in range(2):
            val = both[side * 256 : side * 256 + 128]
            sig = jax.nn.sigmoid(both[side * 256 + 128 : side * 256 + 256])
            vs[side * 2, s] = val
            vs[side * 2 + 1, s] = sig
            stage[pl.ds(side * 8 + s, 128, stride=16), :] = sig * val * m
        return carry

    lax.fori_loop(0, 8, project, 0)
    other = pl.multiple_of((1 - q) * 1024, 1024)
    mine = pl.multiple_of(q * 1024, 1024)
    give1[...] = stage[pl.ds(other, 1024), :].reshape(64, 16, 128).astype(BF16)
    send1[:, pl.ds(q, 1)] = stage[pl.ds(mine, 1024), :].reshape(64, 1, 16, 128).astype(BF16)

    pl.semaphore_wait(bar, 23)
    each_plane(lambda dev, i: signal(ready, dev))
    x1 = remote(give1, send1.at[:, q], X1, sibling)
    x1.start()
    pl.semaphore_wait(ready, 15)
    x1.wait()
    each_owner(lambda dev, o: remote(send1.at[o], got1.at[me], P1, dev).start())

    @pl.when(own)
    def _():
        got1[pl.ds(me, 1)] = send1[pl.ds(chan, 1)]

    load_cot.wait()

    def gates(s, carry):
        n = normed[s]
        g = jax.nn.sigmoid(dot(n, wog[...], 1, 0))
        ct = cells(cin, s)
        do = (ct * g).astype(BF16)
        gate[s] = g
        slope[s] = ct * g * (1.0 - g)
        d_out[pl.ds(pl.multiple_of(s * 128, 128), 128), :] = do
        d_tn[s] = dot(wo[...], do, 1, 1)
        return carry

    lax.fori_loop(0, 8, gates, 0)

    @pl.when(own)
    def _():
        wait_slots(got1, 127, rsem.at[P1])
        for rp in range(4):
            a = got1[rp * 32 : rp * 32 + 16].astype(F32)
            b = got1[rp * 32 + 16 : rp * 32 + 32].astype(F32)
            for part_k, dst in ((0, lk), (8, rk)):
                lo, hi = swap_halves(
                    a[:, :, part_k : part_k + 8].reshape(256, 128), b[:, :, part_k : part_k + 8].reshape(256, 128)
                )
                dst[0:256, rp * 128 : rp * 128 + 128] = lo.astype(BF16)
                dst[256:512, rp * 128 : rp * 128 + 128] = hi.astype(BF16)
        tt[...] = dot(rk[...], lk[...], 0, 0)
        for rp in range(4):
            v = tt[:, rp * 128 : rp * 128 + 128].reshape(8, 2, 32, 128)
            lo, hi = swap_halves(v[:, 0].reshape(256, 128), v[:, 1].reshape(256, 128))
            send2[rp * 32 : rp * 32 + 16] = lo.reshape(16, 16, 128).astype(BF16)
            send2[rp * 32 + 16 : rp * 32 + 32] = hi.reshape(16, 16, 128).astype(BF16)
        each_chip(lambda dev, t: remote(send2.at[t], got2.at[chan], P2, dev).start())
        got2[pl.ds(chan, 1)] = send2[pl.ds(me, 1)]

    wait_owners(got2, rsem.at[P2])

    tri = got2[...].astype(F32)
    first = q == 0
    tri_lo, tri_hi = tri[:, 0:8], tri[:, 8:16]
    give2[...] = jnp.where(first, tri_hi, tri_lo).reshape(32, 16, 128).astype(BF16)
    x2 = remote(give2, take2, X2, sibling)
    x2.start()
    stage[pl.ds(pl.multiple_of(q * 512, 512), 512), :] = jnp.where(first, tri_lo, tri_hi).reshape(512, 128)
    x2.wait()
    stage[pl.ds(pl.multiple_of((1 - q) * 512, 512), 512), :] = take2[...].astype(F32).reshape(512, 128)
    acc[...] = jnp.zeros_like(acc)

    def triangle(s, carry):
        at = pl.ds(s, 128, stride=8)
        t = stage[at, :]
        center = t - jnp.mean(t, axis=0, keepdims=True)
        rstd = lax.rsqrt(jnp.mean(center * center, axis=0, keepdims=True) + EPS)
        hat = center * rstd
        tri_n[s] = (hat * cols[0] + cols[1]).astype(BF16)
        d = d_tn[s]
        dh = d * cols[0]
        mean_dh = jnp.mean(dh, axis=0, keepdims=True)
        mean_dhh = jnp.mean(dh * hat, axis=0, keepdims=True)
        tri_f[at, :] = rstd * (dh - mean_dh - hat * mean_dhh)
        acc[0] += d * hat
        acc[1] += d
        return carry

    lax.fori_loop(0, 8, triangle, 0)
    give3[...] = tri_f[pl.ds(pl.multiple_of((1 - q) * 512, 512), 512), :].reshape(32, 16, 128).astype(BF16)
    x3 = remote(give3, take3, X3, sibling)
    x3.start()
    kept = tri_f[pl.ds(pl.multiple_of(q * 512, 512), 512), :].reshape(64, 8, 128)
    x3.wait()
    came = take3[...].astype(F32).reshape(64, 8, 128)
    send3[...] = jnp.concatenate([jnp.where(first, kept, came), jnp.where(first, came, kept)], axis=1).astype(BF16)
    each_owner(lambda dev, o: remote(send3.at[o], got3.at[me], P3, dev).start())

    @pl.when(own)
    def _():
        got3[pl.ds(me, 1)] = send3[pl.ds(chan, 1)]

    def outputs(s, carry):
        at = pl.ds(pl.multiple_of(s * 128, 128), 128)
        proj = dot(tri_n[s], wo[...], 0, 0)
        cells(update, s, gate[s] * proj)
        dg = (slope[s] * proj).astype(BF16)
        d_gate[at, :] = dg
        dn[s] = dot(dg, wog[...], 1, 1)
        part[512:640, :] += dot(tri_n[s], d_out[at, :], 1, 0)
        part[640:768, :] += dot(normed[s], dg, 0, 0)
        return carry

    part[512:768, :] = jnp.zeros((256, 128), F32)
    lax.fori_loop(0, 8, outputs, 0)

    @pl.when(own)
    def _():
        wait_slots(got3, 127, rsem.at[P3])
        for rp in range(4):
            a = got3[rp * 32 : rp * 32 + 16].astype(F32).reshape(256, 128)
            b = got3[rp * 32 + 16 : rp * 32 + 32].astype(F32).reshape(256, 128)
            lo, hi = swap_halves(a, b)
            dt[:, rp * 128 : rp * 128 + 128] = (
                jnp.concatenate([lo.reshape(8, 1, 32, 128), hi.reshape(8, 1, 32, 128)], axis=1)
                .reshape(512, 128)
                .astype(BF16)
            )
        ol[...] = dot(rk[...], dt[...], 1, 0)
        orr[...] = dot(lk[...], dt[...], 1, 1)
        for rp in range(4):
            lanes = slice(rp * 128, rp * 128 + 128)
            l_lo, l_hi = swap_halves(ol[0:256, lanes], ol[256:512, lanes])
            r_lo, r_hi = swap_halves(orr[0:256, lanes], orr[256:512, lanes])
            shape = (16, 2, 8, 128)
            send4[rp * 32 : rp * 32 + 16] = jnp.concatenate(
                [l_lo.reshape(shape), r_lo.reshape(shape)], axis=2
            ).astype(BF16)
            send4[rp * 32 + 16 : rp * 32 + 32] = jnp.concatenate(
                [l_hi.reshape(shape), r_hi.reshape(shape)], axis=2
            ).astype(BF16)
        each_chip(lambda dev, t: remote(send4.at[t], got4.at[chan], P4, dev).start())
        got4[pl.ds(chan, 1)] = send4[pl.ds(me, 1)]

    wait_owners(got4, rsem.at[P4])
    x4 = remote(got4.at[:, 1 - q], take4, X4, sibling)
    x4.start()
    stage[pl.ds(mine, 1024), :] = got4[:, pl.ds(q, 1)].astype(F32).reshape(1024, 128)
    x4.wait()
    stage[pl.ds(other, 1024), :] = take4[...].astype(F32).reshape(1024, 128)

    def inward(s, carry):
        m = mask[pl.ds(s, 1), :]
        parts = []
        for side in range(2):
            d = stage[pl.ds(side * 8 + s, 128, stride=16), :] * m
            val, sig = vs[side * 2, s], vs[side * 2 + 1, s]
            parts.append((d * sig).astype(BF16))
            parts.append((d * val * sig * (1.0 - sig)).astype(BF16))
        g = jnp.concatenate(parts, axis=0)
        dx[s] = g
        total = dn[s] + dot(g, wcat[...], 0, 1)
        dn[s] = total
        acc[2] += total * hat_in[s]
        acc[3] += total
        part[0:512, :] += dot(g, normed[s], 1, 0)
        return carry

    part[0:512, :] = jnp.zeros((512, 128), F32)
    lax.fori_loop(0, 8, inward, 0)
    norms = jnp.concatenate(
        [
            jnp.sum(acc[2], axis=0, keepdims=True),
            jnp.sum(acc[3], axis=0, keepdims=True),
            jnp.sum(acc[0].T, axis=0, keepdims=True),
            jnp.sum(acc[1].T, axis=0, keepdims=True),
            jnp.zeros((4, 128), F32),
        ],
        axis=0,
    )

    def half(which):
        return jnp.concatenate(
            [
                part[pl.ds(pl.multiple_of(which * 256, 256), 256), :].reshape(16, 16, 128),
                part[pl.ds(pl.multiple_of(512 + which * 128, 128), 128), :].reshape(16, 8, 128),
                jnp.broadcast_to(norms.reshape(1, 8, 128), (16, 8, 128)),
            ],
            axis=1,
        )

    a1_give[...] = half(1 - q).astype(BF16)
    a1 = remote(a1_give, a1_take, A1, sibling)
    a1.start()
    kept_half = half(q)
    a1.wait()
    a2_send[...] = (kept_half + a1_take[...].astype(F32)).astype(BF16)
    each_plane(lambda dev, i: remote(a2_send.at[i], a2_got.at[plane], A2, dev).start())
    a2_got[pl.ds(plane, 1)] = a2_send[pl.ds(plane, 1)]

    def last(s, carry):
        dhat = dn[s] * in_gain[...]
        hat = hat_in[s]
        mean_d = jnp.mean(dhat, axis=-1, keepdims=True)
        mean_dh = jnp.mean(dhat * hat, axis=-1, keepdims=True)
        cells(grad_pair, s, rstd_in[s] * (dhat - mean_d - hat * mean_dh))
        return carry

    lax.fori_loop(0, 4, last, 0)
    wait_slots(a2_got, 15, rsem.at[A2])
    a3_send[...] = jnp.sum(a2_got[...].astype(F32), axis=0)
    each_z(lambda dev, i: remote(a3_send, a3_got.at[z], A3, dev).start())
    a3_got[pl.ds(z, 1)] = a3_send[...].reshape(1, 32, 128)
    lax.fori_loop(4, 8, last, 0)
    wait_slots(a3_got, 7, rsem.at[A3])
    total = jnp.sum(a3_got[...], axis=0) * (1.0 / 512.0)
    g_norms[...] = total[24:28]
    a4_send[...] = total[0:24]
    each_plane(lambda dev, i: remote(a4_send, a4_got.at[plane], A4, dev).start())
    a4_got[pl.ds(plane, 1)] = a4_send[...].reshape(1, 24, 128)
    wait_slots(a4_got, 15, rsem.at[A4])
    a5 = remote(a4_got, a5_take, A5, sibling)
    a5.start()
    a5.wait()
    here, there = a4_got[...], a5_take[...]
    for which, dsts in ((0, (g_left, g_left_gate, g_out)), (1, (g_right, g_right_gate, g_out_gate))):
        piece = jnp.where(q == which, here, there)
        both = piece[:, 0:16].reshape(256, 128)
        dsts[0][...] = both[0:128].T
        dsts[1][...] = both[128:256].T
        dsts[2][...] = piece[:, 16:24].reshape(128, 128)

    wait_owners(send1, ssem.at[P1])
    wait_owners(send3, ssem.at[P3])

    @pl.when(own)
    def _():
        wait_slots(send2, 127, ssem.at[P2])
        wait_slots(send4, 127, ssem.at[P4])

    wait_slots(a2_send, 15, ssem.at[A2])
    wait_slots(a3_got, 7, ssem.at[A3])
    wait_slots(a4_got, 15, ssem.at[A4])


def scratch():
    def v(shape, kind=F32):
        return pltpu.VMEM(shape, kind)

    return [
        v((1024, 128)), v((1024, 128)),
        v((128, 512), BF16), v((512, 128), BF16),
        v((8, 128, 128)), v((8, 128, 1)), v((8, 128, 128), BF16),
        v((4, 8, 128, 128)), v((2048, 128)),
        v((8, 128, 128)), v((8, 128, 128)), v((1024, 128), BF16),
        v((8, 128, 128)), v((8, 128, 128), BF16), v((1024, 128)),
        v((1024, 128), BF16), v((8, 128, 128)), v((8, 512, 128), BF16),
        v((2, 128, 128)), v((4, 128, 128)),
        v((64, 16, 128), BF16), v((64, 2, 16, 128), BF16), v((128, 2, 16, 128), BF16),
        v((512, 512), BF16), v((512, 512), BF16), v((512, 512)),
        v((128, 16, 128), BF16), v((64, 16, 128), BF16),
        v((32, 16, 128), BF16), v((32, 16, 128), BF16),
        v((32, 16, 128), BF16), v((32, 16, 128), BF16),
        v((64, 16, 128), BF16), v((128, 16, 128), BF16),
        v((512, 512), BF16), v((512, 512)), v((512, 512)),
        v((128, 2, 16, 128), BF16), v((64, 2, 16, 128), BF16), v((64, 16, 128), BF16),
        v((768, 128)),
        v((16, 32, 128), BF16), v((16, 32, 128), BF16),
        v((16, 32, 128), BF16), v((16, 32, 128), BF16),
        v((32, 128)), v((8, 32, 128)),
        v((24, 128)), v((16, 24, 128)), v((16, 24, 128)),
        pltpu.SemaphoreType.DMA((2,)),
        pltpu.SemaphoreType.DMA((13,)),
        pltpu.SemaphoreType.DMA((13,)),
        pltpu.SemaphoreType.REGULAR,
    ]


def per_device(
    pair, pair_mask, cotangent, in_gain, in_bias, left_weight, left_gate_weight, right_weight, right_gate_weight,
    out_gain, out_bias, output_weight, output_gate_weight,
):
    mask = pair_mask.astype(F32).reshape(32, 2, 8, 2).transpose(2, 3, 1, 0).reshape(8, 128)
    vm = pl.BlockSpec(memory_space=pltpu.VMEM)
    hbm = pl.BlockSpec(memory_space=pl.ANY)
    square = jax.ShapeDtypeStruct((128, 128), F32)
    cells = jax.ShapeDtypeStruct((1024, 128), F32)
    outs = pl.pallas_call(
        kernel,
        out_shape=(cells, cells) + (square,) * 6 + (jax.ShapeDtypeStruct((4, 128), F32),),
        in_specs=[hbm, hbm] + [vm] * 11,
        out_specs=(vm,) * 9,
        scratch_shapes=scratch(),
        name="triangle",
        compiler_params=pltpu.CompilerParams(
            collective_id=1, has_side_effects=True, vmem_limit_bytes=48 * 1024 * 1024
        ),
    )(
        pair.reshape(1024, 128), cotangent.reshape(1024, 128), mask, in_gain.reshape(1, 128), in_bias.reshape(1, 128),
        left_weight, left_gate_weight, right_weight, right_gate_weight,
        out_gain.reshape(1, 128), out_bias.reshape(1, 128), output_weight, output_gate_weight,
    )
    return (outs[0].reshape(64, 16, 128), outs[1].reshape(64, 16, 128)) + tuple(outs[2:])


def solution(mesh):
    cell, copied = P("row", "col", None), P()
    return jax.shard_map(
        per_device,
        mesh=mesh,
        in_specs=(cell, P("row", "col"), cell) + (copied,) * 10,
        out_specs=(cell, cell) + (copied,) * 7,
        check_vma=False,
    )
```

```python
import functools

import jax
import jax.numpy as jnp
from jax import lax
from jax.experimental import pallas as pl
from jax.experimental.pallas import tpu as pltpu
from jax.sharding import PartitionSpec as P

EPS = 1e-05
MESH = pl.DeviceIdType.MESH
F32, BF16 = jnp.float32, jnp.bfloat16
X1, P1, P2, X2, P3, X3, P4, X4, A1, A2, A3, A4, A5 = range(13)


def dot(a, b, ca, cb):
    return lax.dot_general(a, b, (((ca,), (cb,)), ((), ())), preferred_element_type=F32)


def swap_halves(a, b):
    low = lax.broadcasted_iota(jnp.int32, a.shape, 1) < 64
    return jnp.where(low, a, pltpu.roll(b, 64, 1)), jnp.where(low, pltpu.roll(a, 64, 1), b)


def kernel(
    pair_in, cot_in, mask_in, gi_in, bi_in, wl_in, wlg_in, wr_in, wrg_in, go_in, bo_in, wo_in, wog_in,
    update_out, grad_pair_out, g_weights_out, g_norms_out,
    update, grad_pair, g_weights, g_norms, xin, cin, pair_mask, in_gain, in_bias, wl, wlg, wr, wrg, out_gain, out_bias, wo, wog, mask, wcat, wcat_t, hat_in, rstd_in, normed, vs, stage, gate, slope, d_out, d_tn, tri_n, tri_f, d_gate, dn, dx,
    cols, acc, give1, send1, got1, lk, rk, rk_t, send2, got2, give2, take2, give3, take3, send3, got3, dt,
    send4, got4, take4, part, a1_give, a1_take, a2_send, a2_got, a3_send, a3_got, a4_send, a4_got, a5_take,
    in_sems, out_sems, ssem, rsem, ready,
):
    row, col = lax.axis_index("row"), lax.axis_index("col")
    cc, q = col // 2, col % 2
    x, zl, zh, y = row // 2, row % 2, cc // 4, cc % 4
    z = zh * 2 + zl
    me = row * 16 + cc
    own = row // 4 == q
    not_own = jnp.logical_not(own)
    chan = (row % 4) * 16 + cc
    plane = x * 4 + y
    sibling = (row, cc * 2 + 1 - q)

    def remote(src, dst, k, dev):
        return pltpu.make_async_remote_copy(
            src_ref=src, dst_ref=dst, send_sem=ssem.at[k], recv_sem=rsem.at[k], device_id=dev, device_id_type=MESH
        )

    def wait_slots(buf, n, sem):
        pltpu.make_async_copy(buf.at[pl.ds(0, n)], buf.at[pl.ds(0, n)], sem).wait()

    far = {0: 2, 1: 1, 2: 3, 3: 0}
    offsets = sorted(((dx, dy) for dx in range(4) for dy in range(4)), key=lambda o: -min(o[0], 4 - o[0]) - min(o[1], 4 - o[1]))
    xs, ys = [(x + d) % 4 for d in range(4)], [(y + d) % 4 for d in range(4)]

    def ring(t):
        return (z + 4 + (1 - 2 * (t % 2)) * ((t + 1) // 2)) % 8

    def at_chip(px, py, pz, fn, index=None):
        prow, pcc = px * 2 + pz % 2, pz // 2 * 4 + py
        fn((prow, pcc * 2 + q), prow * 16 + pcc if index is None else index)

    def each_owner(fn):
        sides = (q * 2 + (x + 1) % 2, q * 2 + x % 2)
        targets = [(side, ys[far[d]]) for d in range(4) for side in sides]

        def send(px, py, pz):
            at_chip(px, py, pz, lambda dev, g: fn(dev, g - 64 * q))

        def step(t, carry):
            pz = ring(t)
            for px, py in targets:
                send(px, py, pz)
            return carry

        lax.fori_loop(0, 7, step, 0)
        for px, py in targets[:-1]:
            send(px, py, z)

        @pl.when(not_own)
        def _():
            send(*targets[-1], z)

    def each_plane(fn):
        for dx, dy in offsets[:-1]:
            at_chip(xs[dx], ys[dy], z, fn, xs[dx] * 4 + ys[dy])

    def each_z(fn):
        def step(t, carry):
            pz = ring(t)
            at_chip(x, y, pz, fn, pz)
            return carry

        lax.fori_loop(0, 7, step, 0)

    def wait_owners(buf, sem):
        @pl.when(own)
        def _():
            wait_slots(buf, 63, sem)

        @pl.when(not_own)
        def _():
            wait_slots(buf, 64, sem)

    def signal(sem, dev):
        pl.semaphore_signal(sem, inc=1, device_id=dev, device_id_type=MESH)

    def cells(ref, s, put=None):
        for h in range(4):
            p, par = h // 2, h % 2
            at = pl.ds(par * 16 + 2 * s + p, 32, stride=32)
            if put is not None:
                ref[at, :] = put[h * 32 : h * 32 + 32]
        if put is None:
            return jnp.concatenate(
                [ref[pl.ds(par * 16 + 2 * s + p, 32, stride=32), :] for p in range(2) for par in range(2)], axis=0
            )

    sources = (pair_in, wl_in, wlg_in, wr_in, wrg_in, mask_in, gi_in, bi_in, go_in, bo_in, wo_in, wog_in, cot_in)
    places = (xin, wl, wlg, wr, wrg, pair_mask, in_gain, in_bias, out_gain, out_bias, wo, wog, cin)
    loads = [pltpu.make_async_copy(a, b, in_sems.at[i]) for i, (a, b) in enumerate(zip(sources, places))]
    for load in loads:
        load.start()
    stores = [
        pltpu.make_async_copy(a, b, out_sems.at[i])
        for i, (a, b) in enumerate(
            ((update, update_out), (grad_pair, grad_pair_out), (g_weights, g_weights_out), (g_norms, g_norms_out))
        )
    ]
    bar = pltpu.get_barrier_semaphore()
    signal(bar, sibling)
    each_z(lambda dev, i: signal(bar, dev))
    each_plane(lambda dev, i: signal(bar, dev))

    for load in loads[1:12]:
        load.wait()
    wcat[...] = jnp.concatenate([wl[...], wlg[...], wr[...], wrg[...]], axis=1)
    for i, w in enumerate((wl, wlg, wr, wrg)):
        wcat_t[i * 128 : i * 128 + 128, :] = w[...].astype(F32).T.astype(BF16)
    cols[0] = jnp.broadcast_to(out_gain[...], (128, 128)).T
    cols[1] = jnp.broadcast_to(out_bias[...], (128, 128)).T
    flags = pair_mask[...].astype(F32)
    laid = jnp.zeros((8, 128), F32)
    for p in range(2):
        pick = lax.broadcasted_iota(jnp.int32, (8, 16), 1) == 2 * lax.broadcasted_iota(jnp.int32, (8, 16), 0) + p
        lane = lax.broadcasted_iota(jnp.int32, (64, 128), 1)
        place = jnp.logical_and(
            lane // 64 == p, lax.broadcasted_iota(jnp.int32, (64, 128), 0) == 2 * (lane % 32) + (lane % 64) // 32
        )
        laid += dot(dot(pick.astype(F32), flags, 1, 0), place.astype(F32), 1, 0)
    mask[...] = laid
    loads[0].wait()

    def project(s, carry):
        v = cells(xin, s)
        center = v - jnp.mean(v, axis=-1, keepdims=True)
        rstd = lax.rsqrt(jnp.mean(center * center, axis=-1, keepdims=True) + EPS)
        hat = center * rstd
        n = (hat * in_gain[...] + in_bias[...]).astype(BF16)
        hat_in[s] = hat
        rstd_in[s] = rstd
        normed[s] = n
        both = dot(wcat_t[...], n, 1, 1)
        m = mask[pl.ds(s, 1), :]
        for side in range(2):
            val = both[side * 256 : side * 256 + 128]
            sig = jax.nn.sigmoid(both[side * 256 + 128 : side * 256 + 256])
            vs[side * 2, s] = val
            vs[side * 2 + 1, s] = sig
            stage[pl.ds(side * 8 + s, 128, stride=16), :] = sig * val * m
        return carry

    lax.fori_loop(0, 4, project, 0)
    pl.semaphore_wait(bar, 23)
    each_plane(lambda dev, i: signal(ready, dev))
    lax.fori_loop(4, 8, project, 0)
    other = pl.multiple_of((1 - q) * 1024, 1024)
    mine = pl.multiple_of(q * 1024, 1024)
    give1[...] = stage[pl.ds(other, 1024), :].reshape(64, 16, 128).astype(BF16)
    send1[:, pl.ds(q, 1)] = stage[pl.ds(mine, 1024), :].reshape(64, 1, 16, 128).astype(BF16)

    x1 = remote(give1, send1.at[:, q], X1, sibling)
    x1.start()
    pl.semaphore_wait(ready, 15)
    x1.wait()
    each_owner(lambda dev, o: remote(send1.at[o], got1.at[me], P1, dev).start())

    @pl.when(own)
    def _():
        got1[pl.ds(me, 1)] = send1[pl.ds(chan, 1)]

    loads[12].wait()

    def gates(s, carry):
        n = normed[s]
        g = jax.nn.sigmoid(dot(n, wog[...], 1, 0))
        ct = cells(cin, s)
        do = (ct * g).astype(BF16)
        gate[s] = g
        slope[s] = ct * g * (1.0 - g)
        d_out[pl.ds(pl.multiple_of(s * 128, 128), 128), :] = do
        d_tn[s] = dot(wo[...], do, 1, 1)
        return carry

    lax.fori_loop(0, 8, gates, 0)

    def by_x(block):
        def step(t, carry):
            block((x + 2 + (1 - 2 * (t % 2)) * ((t + 1) // 2)) % 4)
            return carry

        lax.fori_loop(0, 4, step, 0)

    def send_x(px, fn):
        def step(t, carry):
            pz = ring(t)
            for d in range(4):
                at_chip(px, ys[far[d]], pz, fn)
            return carry

        lax.fori_loop(0, 7, step, 0)
        for d in range(3):
            at_chip(px, ys[far[d]], z, fn)

        @pl.when(px != x)
        def _():
            at_chip(px, y, z, fn)

    @pl.when(own)
    def _():
        wait_slots(got1, 127, rsem.at[P1])
        for rp in range(4):
            a = got1[rp * 32 : rp * 32 + 16].astype(F32)
            b = got1[rp * 32 + 16 : rp * 32 + 32].astype(F32)
            for part_k, dst in ((0, lk), (8, rk)):
                lo, hi = swap_halves(
                    a[:, :, part_k : part_k + 8].reshape(256, 128), b[:, :, part_k : part_k + 8].reshape(256, 128)
                )
                dst[0:256, rp * 128 : rp * 128 + 128] = lo.astype(BF16)
                dst[256:512, rp * 128 : rp * 128 + 128] = hi.astype(BF16)
        rk_t[...] = rk[...].astype(F32).T.astype(BF16)

        def block(px):
            lanes = pl.ds(pl.multiple_of(px * 128, 128), 128)
            v = dot(rk_t[...], lk[:, lanes], 1, 0).reshape(8, 2, 32, 128)
            lo, hi = swap_halves(v[:, 0].reshape(256, 128), v[:, 1].reshape(256, 128))
            send2[pl.ds(px * 32, 16)] = lo.reshape(16, 16, 128).astype(BF16)
            send2[pl.ds(px * 32 + 16, 16)] = hi.reshape(16, 16, 128).astype(BF16)
            send_x(px, lambda dev, t: remote(send2.at[t], got2.at[chan], P2, dev).start())

        by_x(block)
        got2[pl.ds(chan, 1)] = send2[pl.ds(me, 1)]

    wait_owners(got2, rsem.at[P2])

    tri = got2[...].astype(F32)
    first = q == 0
    tri_lo, tri_hi = tri[:, 0:8], tri[:, 8:16]
    give2[...] = jnp.where(first, tri_hi, tri_lo).reshape(32, 16, 128).astype(BF16)
    x2 = remote(give2, take2, X2, sibling)
    x2.start()
    stage[pl.ds(pl.multiple_of(q * 512, 512), 512), :] = jnp.where(first, tri_lo, tri_hi).reshape(512, 128)
    x2.wait()
    stage[pl.ds(pl.multiple_of((1 - q) * 512, 512), 512), :] = take2[...].astype(F32).reshape(512, 128)
    acc[...] = jnp.zeros_like(acc)

    def triangle(s, carry):
        at = pl.ds(s, 128, stride=8)
        t = stage[at, :]
        center = t - jnp.mean(t, axis=0, keepdims=True)
        rstd = lax.rsqrt(jnp.mean(center * center, axis=0, keepdims=True) + EPS)
        hat = center * rstd
        tri_n[s] = (hat * cols[0] + cols[1]).astype(BF16)
        d = d_tn[s]
        dh = d * cols[0]
        mean_dh = jnp.mean(dh, axis=0, keepdims=True)
        mean_dhh = jnp.mean(dh * hat, axis=0, keepdims=True)
        tri_f[at, :] = rstd * (dh - mean_dh - hat * mean_dhh)
        acc[0] += d * hat
        acc[1] += d
        return carry

    lax.fori_loop(0, 8, triangle, 0)
    give3[...] = tri_f[pl.ds(pl.multiple_of((1 - q) * 512, 512), 512), :].reshape(32, 16, 128).astype(BF16)
    x3 = remote(give3, take3, X3, sibling)
    x3.start()
    kept = tri_f[pl.ds(pl.multiple_of(q * 512, 512), 512), :].reshape(64, 8, 128)
    x3.wait()
    came = take3[...].astype(F32).reshape(64, 8, 128)
    send3[...] = jnp.concatenate([jnp.where(first, kept, came), jnp.where(first, came, kept)], axis=1).astype(BF16)
    each_owner(lambda dev, o: remote(send3.at[o], got3.at[me], P3, dev).start())

    @pl.when(own)
    def _():
        got3[pl.ds(me, 1)] = send3[pl.ds(chan, 1)]

    def outputs(s, carry):
        at = pl.ds(pl.multiple_of(s * 128, 128), 128)
        proj = dot(tri_n[s], wo[...], 0, 0)
        cells(update, s, gate[s] * proj)
        dg = (slope[s] * proj).astype(BF16)
        d_gate[at, :] = dg
        dn[s] = dot(dg, wog[...], 1, 1)
        part[512:640, :] += dot(tri_n[s], d_out[at, :], 1, 0)
        part[640:768, :] += dot(normed[s], dg, 0, 0)
        return carry

    part[512:768, :] = jnp.zeros((256, 128), F32)
    lax.fori_loop(0, 8, outputs, 0)
    stores[0].start()

    @pl.when(own)
    def _():
        wait_slots(got3, 127, rsem.at[P3])
        for rp in range(4):
            a = got3[rp * 32 : rp * 32 + 16].astype(F32).reshape(256, 128)
            b = got3[rp * 32 + 16 : rp * 32 + 32].astype(F32).reshape(256, 128)
            lo, hi = swap_halves(a, b)
            dt[:, rp * 128 : rp * 128 + 128] = (
                jnp.concatenate([lo.reshape(8, 1, 32, 128), hi.reshape(8, 1, 32, 128)], axis=1)
                .reshape(512, 128)
                .astype(BF16)
            )

        def block(px):
            lanes = pl.ds(pl.multiple_of(px * 128, 128), 128)
            left = dot(rk[...], dt[:, lanes], 1, 0)
            right = dot(lk[...], dt[lanes, :], 1, 1)
            l_lo, l_hi = swap_halves(left[0:256], left[256:512])
            r_lo, r_hi = swap_halves(right[0:256], right[256:512])
            shape = (16, 2, 8, 128)
            send4[pl.ds(px * 32, 16)] = jnp.concatenate([l_lo.reshape(shape), r_lo.reshape(shape)], axis=2).astype(BF16)
            send4[pl.ds(px * 32 + 16, 16)] = jnp.concatenate(
                [l_hi.reshape(shape), r_hi.reshape(shape)], axis=2
            ).astype(BF16)
            send_x(px, lambda dev, t: remote(send4.at[t], got4.at[chan], P4, dev).start())

        by_x(block)
        got4[pl.ds(chan, 1)] = send4[pl.ds(me, 1)]

    wait_owners(got4, rsem.at[P4])
    x4 = remote(got4.at[:, 1 - q], take4, X4, sibling)
    x4.start()
    stage[pl.ds(mine, 1024), :] = got4[:, pl.ds(q, 1)].astype(F32).reshape(1024, 128)
    x4.wait()
    stage[pl.ds(other, 1024), :] = take4[...].astype(F32).reshape(1024, 128)

    def inward(s, carry):
        m = mask[pl.ds(s, 1), :]
        parts = []
        for side in range(2):
            d = stage[pl.ds(side * 8 + s, 128, stride=16), :] * m
            val, sig = vs[side * 2, s], vs[side * 2 + 1, s]
            parts.append((d * sig).astype(BF16))
            parts.append((d * val * sig * (1.0 - sig)).astype(BF16))
        g = jnp.concatenate(parts, axis=0)
        dx[s] = g
        total = dn[s] + dot(g, wcat[...], 0, 1)
        dn[s] = total
        acc[2] += total * hat_in[s]
        acc[3] += total
        part[0:512, :] += dot(g, normed[s], 1, 0)
        return carry

    part[0:512, :] = jnp.zeros((512, 128), F32)
    lax.fori_loop(0, 8, inward, 0)
    norms = jnp.concatenate(
        [
            jnp.sum(acc[2], axis=0, keepdims=True),
            jnp.sum(acc[3], axis=0, keepdims=True),
            jnp.sum(acc[0].T, axis=0, keepdims=True),
            jnp.sum(acc[1].T, axis=0, keepdims=True),
            jnp.zeros((4, 128), F32),
        ],
        axis=0,
    )

    def half(which):
        return jnp.concatenate(
            [
                part[pl.ds(pl.multiple_of(which * 256, 256), 256), :].reshape(16, 16, 128),
                part[pl.ds(pl.multiple_of(512 + which * 128, 128), 128), :].reshape(16, 8, 128),
                jnp.broadcast_to(norms.reshape(1, 8, 128), (16, 8, 128)),
            ],
            axis=1,
        )

    a1_give[...] = half(1 - q).astype(BF16)
    a1 = remote(a1_give, a1_take, A1, sibling)
    a1.start()
    kept_half = half(q)
    a1.wait()
    a2_send[...] = (kept_half + a1_take[...].astype(F32)).astype(BF16)
    each_plane(lambda dev, i: remote(a2_send.at[i], a2_got.at[plane], A2, dev).start())
    a2_got[pl.ds(plane, 1)] = a2_send[pl.ds(plane, 1)]

    def last(s, carry):
        dhat = dn[s] * in_gain[...]
        hat = hat_in[s]
        mean_d = jnp.mean(dhat, axis=-1, keepdims=True)
        mean_dh = jnp.mean(dhat * hat, axis=-1, keepdims=True)
        cells(grad_pair, s, rstd_in[s] * (dhat - mean_d - hat * mean_dh))
        return carry

    lax.fori_loop(0, 4, last, 0)
    wait_slots(a2_got, 15, rsem.at[A2])
    a3_send[...] = jnp.sum(a2_got[...].astype(F32), axis=0).astype(BF16)
    each_z(lambda dev, i: remote(a3_send, a3_got.at[z], A3, dev).start())
    a3_got[pl.ds(z, 1)] = a3_send[...].reshape(1, 32, 128)
    lax.fori_loop(4, 8, last, 0)
    stores[1].start()
    wait_slots(a3_got, 7, rsem.at[A3])
    total = jnp.sum(a3_got[...].astype(F32), axis=0) * (1.0 / 512.0)
    g_norms[...] = total[24:32]
    a4_send[...] = total.astype(BF16)
    each_plane(lambda dev, i: remote(a4_send, a4_got.at[plane], A4, dev).start())
    a4_got[pl.ds(plane, 1)] = a4_send[...].reshape(1, 32, 128)
    wait_slots(a4_got, 15, rsem.at[A4])
    a5 = remote(a4_got, a5_take, A5, sibling)
    a5.start()
    a5.wait()
    here, there = a4_got[...].astype(F32), a5_take[...].astype(F32)
    for which in range(2):
        piece = jnp.where(q == which, here, there)
        both = piece[:, 0:16].reshape(256, 128)
        g_weights[which * 2] = both[0:128].T
        g_weights[which * 2 + 1] = both[128:256].T
        g_weights[4 + which] = piece[:, 16:24].reshape(128, 128)

    stores[2].start()
    stores[3].start()
    wait_owners(send1, ssem.at[P1])
    wait_owners(send3, ssem.at[P3])

    @pl.when(own)
    def _():
        wait_slots(send2, 127, ssem.at[P2])
        wait_slots(send4, 127, ssem.at[P4])

    wait_slots(a2_send, 15, ssem.at[A2])
    wait_slots(a3_got, 7, ssem.at[A3])
    wait_slots(a4_got, 15, ssem.at[A4])
    for store in stores:
        store.wait()


def hand_out(update, grad_pair, g_weights, g_norms, *refs):
    outs, held, in_sems, sems = refs[:9], refs[9:13], refs[13], refs[14]
    loads = [
        pltpu.make_async_copy(a, b, in_sems.at[i])
        for i, (a, b) in enumerate(zip((update, grad_pair, g_weights, g_norms), held))
    ]
    sources = [held[0], held[1]] + [held[2].at[i] for i in range(6)] + [held[3].at[pl.ds(0, 4)]]
    copies = [pltpu.make_async_copy(a, b, sems.at[i]) for i, (a, b) in enumerate(zip(sources, outs))]
    for load in loads:
        load.start()
    for load, part in zip(loads, (copies[0:1], copies[1:2], copies[2:8], copies[8:9])):
        load.wait()
        for copy in part:
            copy.start()
    for copy in copies:
        copy.wait()


def scratch():
    def v(shape, kind=F32):
        return pltpu.VMEM(shape, kind)

    return [
        v((1024, 128)), v((1024, 128)), v((6, 128, 128)), v((8, 128)),
        v((1024, 128)), v((1024, 128)), v((16, 64), jnp.int32), v((1, 128)), v((1, 128)),
        v((128, 128), BF16), v((128, 128), BF16), v((128, 128), BF16), v((128, 128), BF16),
        v((1, 128)), v((1, 128)), v((128, 128), BF16), v((128, 128), BF16), v((8, 128)),
        v((128, 512), BF16), v((512, 128), BF16),
        v((8, 128, 128)), v((8, 128, 1)), v((8, 128, 128), BF16),
        v((4, 8, 128, 128)), v((2048, 128)),
        v((8, 128, 128)), v((8, 128, 128)), v((1024, 128), BF16),
        v((8, 128, 128)), v((8, 128, 128), BF16), v((1024, 128)),
        v((1024, 128), BF16), v((8, 128, 128)), v((8, 512, 128), BF16),
        v((2, 128, 128)), v((4, 128, 128)),
        v((64, 16, 128), BF16), v((64, 2, 16, 128), BF16), v((128, 2, 16, 128), BF16),
        v((512, 512), BF16), v((512, 512), BF16), v((512, 512), BF16),
        v((128, 16, 128), BF16), v((64, 16, 128), BF16),
        v((32, 16, 128), BF16), v((32, 16, 128), BF16),
        v((32, 16, 128), BF16), v((32, 16, 128), BF16),
        v((64, 16, 128), BF16), v((128, 16, 128), BF16),
        v((512, 512), BF16),
        v((128, 2, 16, 128), BF16), v((64, 2, 16, 128), BF16), v((64, 16, 128), BF16),
        v((768, 128)),
        v((16, 32, 128), BF16), v((16, 32, 128), BF16),
        v((16, 32, 128), BF16), v((16, 32, 128), BF16),
        v((32, 128), BF16), v((8, 32, 128), BF16),
        v((32, 128), BF16), v((16, 32, 128), BF16), v((16, 32, 128), BF16),
        pltpu.SemaphoreType.DMA((13,)),
        pltpu.SemaphoreType.DMA((4,)),
        pltpu.SemaphoreType.DMA((13,)),
        pltpu.SemaphoreType.DMA((13,)),
        pltpu.SemaphoreType.REGULAR,
    ]


def per_device(
    pair, pair_mask, cotangent, in_gain, in_bias, left_weight, left_gate_weight, right_weight, right_gate_weight,
    out_gain, out_bias, output_weight, output_gate_weight,
):
    hbm = pl.BlockSpec(memory_space=pl.ANY)
    square = jax.ShapeDtypeStruct((128, 128), F32)
    cells = jax.ShapeDtypeStruct((1024, 128), F32)
    found = pl.pallas_call(
        kernel,
        out_shape=(cells, cells, jax.ShapeDtypeStruct((6, 128, 128), F32), jax.ShapeDtypeStruct((8, 128), F32)),
        in_specs=[hbm] * 13,
        out_specs=(hbm,) * 4,
        scratch_shapes=scratch(),
        name="triangle",
        compiler_params=pltpu.CompilerParams(
            collective_id=1, has_side_effects=True, vmem_limit_bytes=60 * 1024 * 1024
        ),
    )(
        pair.reshape(1024, 128), cotangent.reshape(1024, 128), pair_mask.T, in_gain.reshape(1, 128), in_bias.reshape(1, 128),
        left_weight, left_gate_weight, right_weight, right_gate_weight,
        out_gain.reshape(1, 128), out_bias.reshape(1, 128), output_weight, output_gate_weight,
    )
    outs = pl.pallas_call(
        hand_out,
        out_shape=(cells, cells) + (square,) * 6 + (jax.ShapeDtypeStruct((4, 128), F32),),
        in_specs=[hbm] * 4,
        out_specs=(hbm,) * 9,
        scratch_shapes=[
            pltpu.VMEM((1024, 128), F32),
            pltpu.VMEM((1024, 128), F32),
            pltpu.VMEM((6, 128, 128), F32),
            pltpu.VMEM((8, 128), F32),
            pltpu.SemaphoreType.DMA((4,)),
            pltpu.SemaphoreType.DMA((9,)),
        ],
        name="hand_out",
        compiler_params=pltpu.CompilerParams(vmem_limit_bytes=60 * 1024 * 1024),
    )(*found)
    return (outs[0].reshape(64, 16, 128), outs[1].reshape(64, 16, 128)) + tuple(outs[2:])


def solution(mesh):
    cell, copied = P("row", "col", None), P()
    return jax.shard_map(
        per_device,
        mesh=mesh,
        in_specs=(cell, P("row", "col"), cell) + (copied,) * 10,
        out_specs=(cell, cell) + (copied,) * 7,
        check_vma=False,
    )
```

```python
import functools

import jax
import jax.numpy as jnp
from jax import lax
from jax.experimental import pallas as pl
from jax.experimental.pallas import tpu as pltpu
from jax.sharding import PartitionSpec as P

EPS = 1e-05
MESH = pl.DeviceIdType.MESH
F32, BF16 = jnp.float32, jnp.bfloat16
X1, X1B, P1, P2, P2B, X2, X2B, P3, X3, X3B, P4, P4B, X4, X4B, A2, A3, A4 = range(17)


def dot(a, b, ca, cb):
    return lax.dot_general(a, b, (((ca,), (cb,)), ((), ())), preferred_element_type=F32)


def swap_halves(a, b):
    low = lax.broadcasted_iota(jnp.int32, a.shape, 1) < 64
    return jnp.where(low, a, pltpu.roll(b, 64, 1)), jnp.where(low, pltpu.roll(a, 64, 1), b)


def kernel(
    pair_in, cot_in, mask_in, gi_in, bi_in, wl_in, wlg_in, wr_in, wrg_in, go_in, bo_in, wo_in, wog_in,
    update_out, grad_pair_out, g_weights_out, g_norms_out,
    update, grad_pair, g_weights, g_norms, xin, cin, pair_mask, in_gain, in_bias, wl, wlg, wr, wrg, out_gain, out_bias, wo, wog, mask, wcat, wcat_t, hat_in, rstd_in, normed, vs, stage, gate, slope, d_out, d_tn, tri_n, tri_f, d_gate, dn, dx,
    cols, acc, give1, send1, got1, lk, rk, rk_t, send2, got2, give2, take2, give3, take3, send3, got3, dt,
    send4, got4, take4, part, a2_send, a2_got, a3_send, a3_got, a4_send, a4_got,
    in_sems, out_sems, ssem, rsem, ready,
):
    row, col = lax.axis_index("row"), lax.axis_index("col")
    cc, q = col // 2, col % 2
    x, zl, zh, y = row // 2, row % 2, cc // 4, cc % 4
    z = zh * 2 + zl
    me = row * 16 + cc
    own = row // 4 == q
    not_own = jnp.logical_not(own)
    chan = zl * 32 + x % 2 * 16 + cc
    plane = x * 4 + y
    sibling = (row, cc * 2 + 1 - q)

    def remote(src, dst, k, dev):
        return pltpu.make_async_remote_copy(
            src_ref=src, dst_ref=dst, send_sem=ssem.at[k], recv_sem=rsem.at[k], device_id=dev, device_id_type=MESH
        )

    def wait_slots(buf, n, sem):
        pltpu.make_async_copy(buf.at[pl.ds(0, n)], buf.at[pl.ds(0, n)], sem).wait()

    far = {0: 2, 1: 1, 2: 3, 3: 0}
    offsets = sorted(((dx, dy) for dx in range(4) for dy in range(4)), key=lambda o: -min(o[0], 4 - o[0]) - min(o[1], 4 - o[1]))
    xs, ys = [(x + d) % 4 for d in range(4)], [(y + d) % 4 for d in range(4)]

    def ring(t):
        return (z + 4 + (1 - 2 * (t % 2)) * ((t + 1) // 2)) % 8

    def at_chip(px, py, pz, fn, index=None):
        prow, pcc = px * 2 + pz % 2, pz // 2 * 4 + py
        fn((prow, pcc * 2 + q), prow * 16 + pcc if index is None else index)

    def by_x(block):
        def step(t, carry):
            block((x + 2 + (1 - 2 * (t % 2)) * ((t + 1) // 2)) % 4)
            return carry

        lax.fori_loop(0, 4, step, 0)

    def send_half(half, fn):
        sides = (q * 2 + (x + 1) % 2, q * 2 + x % 2)
        targets = [(side, ys[far[d]]) for d in range(4) for side in sides]

        def step(t, carry):
            pz = (z + 4 + (1 - 2 * (t % 2)) * ((t + 1) // 2) * 2 + (z + half) % 2) % 8
            for px, py in targets:
                at_chip(px, py, pz, lambda dev, g: fn(dev, half * 32 + px % 2 * 16 + g % 16))
            return carry

        lax.fori_loop(0, 3, step, 0)
        pz = (z + (z + half) % 2) % 8
        for px, py in targets[:-1]:
            at_chip(px, py, pz, lambda dev, g: fn(dev, half * 32 + px % 2 * 16 + g % 16))

        @pl.when(jnp.logical_or(not_own, zl != half))
        def _():
            px, py = targets[-1]
            at_chip(px, py, pz, lambda dev, g: fn(dev, half * 32 + px % 2 * 16 + g % 16))

    def send_x(px, fn):
        def step(t, carry):
            pz = ring(t)
            for d in range(4):
                at_chip(px, ys[far[d]], pz, fn)
            return carry

        lax.fori_loop(0, 7, step, 0)
        for d in range(3):
            at_chip(px, ys[far[d]], z, fn)

        @pl.when(px != x)
        def _():
            at_chip(px, y, z, fn)

    def each_plane(fn):
        for dx, dy in offsets[:-1]:
            at_chip(xs[dx], ys[dy], z, fn, xs[dx] * 4 + ys[dy])

    def each_z(fn):
        def step(t, carry):
            pz = ring(t)
            at_chip(x, y, pz, fn, pz)
            return carry

        lax.fori_loop(0, 7, step, 0)

    def wait_owners(buf, sem):
        @pl.when(own)
        def _():
            wait_slots(buf, 63, sem)

        @pl.when(not_own)
        def _():
            wait_slots(buf, 64, sem)

    def wait_half(buf, half, sem):
        mine_too = jnp.logical_and(own, zl == half)

        @pl.when(mine_too)
        def _():
            wait_slots(buf, 31, sem)

        @pl.when(jnp.logical_not(mine_too))
        def _():
            wait_slots(buf, 32, sem)

    def signal(sem, dev):
        pl.semaphore_signal(sem, inc=1, device_id=dev, device_id_type=MESH)

    def cells(ref, s, put=None):
        for h in range(4):
            p, par = h // 2, h % 2
            at = pl.ds(par * 16 + 2 * s + p, 32, stride=32)
            if put is not None:
                ref[at, :] = put[h * 32 : h * 32 + 32]
        if put is None:
            return jnp.concatenate(
                [ref[pl.ds(par * 16 + 2 * s + p, 32, stride=32), :] for p in range(2) for par in range(2)], axis=0
            )

    sources = (pair_in, wl_in, wlg_in, wr_in, wrg_in, mask_in, gi_in, bi_in, go_in, bo_in, wo_in, wog_in, cot_in)
    places = (xin, wl, wlg, wr, wrg, pair_mask, in_gain, in_bias, out_gain, out_bias, wo, wog, cin)
    loads = [pltpu.make_async_copy(a, b, in_sems.at[i]) for i, (a, b) in enumerate(zip(sources, places))]
    for load in loads:
        load.start()
    stores = [
        pltpu.make_async_copy(a, b, out_sems.at[i])
        for i, (a, b) in enumerate(
            ((update, update_out), (grad_pair, grad_pair_out), (g_weights, g_weights_out), (g_norms, g_norms_out))
        )
    ]
    bar = pltpu.get_barrier_semaphore()
    signal(bar, sibling)
    each_z(lambda dev, i: signal(bar, dev))
    each_plane(lambda dev, i: signal(bar, dev))

    for load in (loads[0], loads[6], loads[7]):
        load.wait()

    def center(s, carry):
        v = cells(xin, s)
        middle = v - jnp.mean(v, axis=-1, keepdims=True)
        rstd = lax.rsqrt(jnp.mean(middle * middle, axis=-1, keepdims=True) + EPS)
        hat = middle * rstd
        hat_in[s] = hat
        rstd_in[s] = rstd
        normed[s] = (hat * in_gain[...] + in_bias[...]).astype(BF16)
        return carry

    lax.fori_loop(0, 8, center, 0)
    for load in loads[1:6] + loads[8:12]:
        load.wait()
    for i, w in enumerate((wl, wlg, wr, wrg)):
        turned = w[...].astype(F32).T.astype(BF16)
        for half in range(2):
            for core in range(2):
                to = half * 256 + i * 64 + core * 32
                wcat_t[to : to + 32, :] = turned[core * 64 + half * 32 : core * 64 + half * 32 + 32]
    flags = pair_mask[...].astype(F32)
    laid = jnp.zeros((8, 128), F32)
    for p in range(2):
        pick = lax.broadcasted_iota(jnp.int32, (8, 16), 1) == 2 * lax.broadcasted_iota(jnp.int32, (8, 16), 0) + p
        lane = lax.broadcasted_iota(jnp.int32, (64, 128), 1)
        place = jnp.logical_and(
            lane // 64 == p, lax.broadcasted_iota(jnp.int32, (64, 128), 0) == 2 * (lane % 32) + (lane % 64) // 32
        )
        laid += dot(dot(pick.astype(F32), flags, 1, 0), place.astype(F32), 1, 0)
    mask[...] = laid
    pl.semaphore_wait(bar, 23)
    each_plane(lambda dev, i: signal(ready, dev))

    def project(half):
        def step(s, carry):
            both = dot(wcat_t[half * 256 : half * 256 + 256, :], normed[s], 1, 1)
            m = mask[pl.ds(s, 1), :]
            for side in range(2):
                val = both[side * 128 : side * 128 + 64]
                sig = jax.nn.sigmoid(both[side * 128 + 64 : side * 128 + 128])
                value = sig * val * m
                for core in range(2):
                    start = core * 64 + half * 32
                    rows = slice(core * 32, core * 32 + 32)
                    vs[side * 2, s, pl.ds(start, 32), :] = val[rows]
                    vs[side * 2 + 1, s, pl.ds(start, 32), :] = sig[rows]
                    stage[pl.ds(start * 16 + side * 8 + s, 32, stride=16), :] = value[rows]
            return carry

        lax.fori_loop(0, 8, step, 0)
        to = pl.ds(half * 32, 32)
        theirs = pl.ds(pl.multiple_of((1 - q) * 1024 + half * 512, 512), 512)
        ours = pl.ds(pl.multiple_of(q * 1024 + half * 512, 512), 512)
        give1[to] = stage[theirs, :].reshape(32, 16, 128).astype(BF16)
        send1[to, pl.ds(q, 1)] = stage[ours, :].reshape(32, 1, 16, 128).astype(BF16)
        copy = remote(give1.at[pl.ds(half * 32, 32)], send1.at[pl.ds(half * 32, 32), q], (X1, X1B)[half], sibling)
        copy.start()
        return copy

    x1 = [project(0), project(1)]
    other = pl.multiple_of((1 - q) * 1024, 1024)
    mine = pl.multiple_of(q * 1024, 1024)
    pl.semaphore_wait(ready, 15)
    for half in range(2):
        x1[half].wait()
        send_half(half, lambda dev, c: remote(send1.at[c], got1.at[me], P1, dev).start())

    @pl.when(own)
    def _():
        got1[pl.ds(me, 1)] = send1[pl.ds(chan, 1)]

    @pl.when(own)
    def _():
        wait_slots(got1, 127, rsem.at[P1])
        for rp in range(4):
            a = got1[rp * 32 : rp * 32 + 16].astype(F32)
            b = got1[rp * 32 + 16 : rp * 32 + 32].astype(F32)
            for part_k, dst in ((0, lk), (8, rk)):
                lo, hi = swap_halves(
                    a[:, :, part_k : part_k + 8].reshape(256, 128), b[:, :, part_k : part_k + 8].reshape(256, 128)
                )
                dst[0:256, rp * 128 : rp * 128 + 128] = lo.astype(BF16)
                dst[256:512, rp * 128 : rp * 128 + 128] = hi.astype(BF16)
        rk_t[...] = rk[...].astype(F32).T.astype(BF16)

        def block(px):
            lanes = pl.ds(pl.multiple_of(px * 128, 128), 128)
            v = dot(rk_t[...], lk[:, lanes], 1, 0).reshape(8, 2, 32, 128)
            lo, hi = swap_halves(v[:, 0].reshape(256, 128), v[:, 1].reshape(256, 128))
            send2[pl.ds(px * 32, 16)] = lo.reshape(16, 16, 128).astype(BF16)
            send2[pl.ds(px * 32 + 16, 16)] = hi.reshape(16, 16, 128).astype(BF16)
            send_x(px, lambda dev, t: remote(send2.at[t], got2.at[chan], P2 + zl, dev).start())

        by_x(block)
        got2[pl.ds(chan, 1)] = send2[pl.ds(me, 1)]

    loads[12].wait()
    wcat[...] = jnp.concatenate([wl[...], wlg[...], wr[...], wrg[...]], axis=1)
    cols[0] = jnp.broadcast_to(out_gain[...], (128, 128)).T
    cols[1] = jnp.broadcast_to(out_bias[...], (128, 128)).T

    def gates(s, carry):
        n = normed[s]
        g = jax.nn.sigmoid(dot(n, wog[...], 1, 0))
        ct = cells(cin, s)
        do = (ct * g).astype(BF16)
        gate[s] = g
        slope[s] = ct * g * (1.0 - g)
        d_out[pl.ds(pl.multiple_of(s * 128, 128), 128), :] = do
        d_tn[s] = dot(wo[...], do, 1, 1)
        return carry

    lax.fori_loop(0, 8, gates, 0)

    first = q == 0
    x2 = []
    for half in range(2):
        wait_half(got2, half, rsem.at[(P2, P2B)[half]])
        tri = got2[half * 32 : half * 32 + 32].astype(F32)
        tri_lo, tri_hi = tri[:, 0:8], tri[:, 8:16]
        part2 = pl.ds(half * 16, 16)
        give2[part2] = jnp.where(first, tri_hi, tri_lo).reshape(16, 16, 128).astype(BF16)
        x2.append(remote(give2.at[part2], take2.at[part2], (X2, X2B)[half], sibling))
        x2[half].start()
        ours = pl.ds(pl.multiple_of(q * 512 + half * 256, 256), 256)
        stage[ours, :] = jnp.where(first, tri_lo, tri_hi).reshape(256, 128)
    for half in range(2):
        x2[half].wait()
        theirs = pl.ds(pl.multiple_of((1 - q) * 512 + half * 256, 256), 256)
        stage[theirs, :] = take2[half * 16 : half * 16 + 16].astype(F32).reshape(256, 128)
    acc[...] = jnp.zeros_like(acc)

    def triangle(s, carry):
        at = pl.ds(s, 128, stride=8)
        t = stage[at, :]
        center = t - jnp.mean(t, axis=0, keepdims=True)
        rstd = lax.rsqrt(jnp.mean(center * center, axis=0, keepdims=True) + EPS)
        hat = center * rstd
        tri_n[s] = (hat * cols[0] + cols[1]).astype(BF16)
        d = d_tn[s]
        dh = d * cols[0]
        mean_dh = jnp.mean(dh, axis=0, keepdims=True)
        mean_dhh = jnp.mean(dh * hat, axis=0, keepdims=True)
        tri_f[at, :] = rstd * (dh - mean_dh - hat * mean_dhh)
        acc[0] += d * hat
        acc[1] += d
        return carry

    lax.fori_loop(0, 8, triangle, 0)
    x3 = []
    for half in range(2):
        theirs = pl.ds(pl.multiple_of((1 - q) * 512 + half * 256, 256), 256)
        part3 = pl.ds(half * 16, 16)
        give3[part3] = tri_f[theirs, :].reshape(16, 16, 128).astype(BF16)
        x3.append(remote(give3.at[part3], take3.at[part3], (X3, X3B)[half], sibling))
        x3[half].start()
    for half in range(2):
        kept = tri_f[pl.ds(pl.multiple_of(q * 512 + half * 256, 256), 256), :].reshape(32, 8, 128)
        x3[half].wait()
        came = take3[pl.ds(half * 16, 16)].astype(F32).reshape(32, 8, 128)
        send3[pl.ds(half * 32, 32)] = jnp.concatenate(
            [jnp.where(first, kept, came), jnp.where(first, came, kept)], axis=1
        ).astype(BF16)
        send_half(half, lambda dev, c: remote(send3.at[c], got3.at[me], P3, dev).start())

    @pl.when(own)
    def _():
        got3[pl.ds(me, 1)] = send3[pl.ds(chan, 1)]

    @pl.when(own)
    def _():
        wait_slots(got3, 127, rsem.at[P3])
        for rp in range(4):
            a = got3[rp * 32 : rp * 32 + 16].astype(F32).reshape(256, 128)
            b = got3[rp * 32 + 16 : rp * 32 + 32].astype(F32).reshape(256, 128)
            lo, hi = swap_halves(a, b)
            dt[:, rp * 128 : rp * 128 + 128] = (
                jnp.concatenate([lo.reshape(8, 1, 32, 128), hi.reshape(8, 1, 32, 128)], axis=1)
                .reshape(512, 128)
                .astype(BF16)
            )

        def block(px):
            lanes = pl.ds(pl.multiple_of(px * 128, 128), 128)
            left = dot(rk[...], dt[:, lanes], 1, 0)
            right = dot(lk[...], dt[lanes, :], 1, 1)
            l_lo, l_hi = swap_halves(left[0:256], left[256:512])
            r_lo, r_hi = swap_halves(right[0:256], right[256:512])
            shape = (16, 2, 8, 128)
            send4[pl.ds(px * 32, 16)] = jnp.concatenate([l_lo.reshape(shape), r_lo.reshape(shape)], axis=2).astype(BF16)
            send4[pl.ds(px * 32 + 16, 16)] = jnp.concatenate(
                [l_hi.reshape(shape), r_hi.reshape(shape)], axis=2
            ).astype(BF16)
            send_x(px, lambda dev, t: remote(send4.at[t], got4.at[chan], P4 + zl, dev).start())

        by_x(block)
        got4[pl.ds(chan, 1)] = send4[pl.ds(me, 1)]

    def outputs(s, carry):
        at = pl.ds(pl.multiple_of(s * 128, 128), 128)
        proj = dot(tri_n[s], wo[...], 0, 0)
        cells(update, s, gate[s] * proj)
        dg = (slope[s] * proj).astype(BF16)
        d_gate[at, :] = dg
        dn[s] = dot(dg, wog[...], 1, 1)
        part[512:640, :] += dot(tri_n[s], d_out[at, :], 1, 0)
        part[640:768, :] += dot(normed[s], dg, 0, 0)
        return carry

    part[512:768, :] = jnp.zeros((256, 128), F32)
    lax.fori_loop(0, 8, outputs, 0)
    stores[0].start()

    x4 = []
    for half in range(2):
        wait_half(got4, half, rsem.at[(P4, P4B)[half]])
        part4 = pl.ds(half * 32, 32)
        x4.append(remote(got4.at[part4, 1 - q], take4.at[part4], (X4, X4B)[half], sibling))
        x4[half].start()
        ours = pl.ds(pl.multiple_of(q * 1024 + half * 512, 512), 512)
        stage[ours, :] = got4[part4, pl.ds(q, 1)].astype(F32).reshape(512, 128)
    for half in range(2):
        x4[half].wait()
        theirs = pl.ds(pl.multiple_of((1 - q) * 1024 + half * 512, 512), 512)
        stage[theirs, :] = take4[half * 32 : half * 32 + 32].astype(F32).reshape(512, 128)
    def inward(s, carry):
        m = mask[pl.ds(s, 1), :]
        parts = []
        for side in range(2):
            d = stage[pl.ds(side * 8 + s, 128, stride=16), :] * m
            val, sig = vs[side * 2, s], vs[side * 2 + 1, s]
            parts.append((d * sig).astype(BF16))
            parts.append((d * val * sig * (1.0 - sig)).astype(BF16))
        g = jnp.concatenate(parts, axis=0)
        dx[s] = g
        total = dn[s] + dot(g, wcat[...], 0, 1)
        dn[s] = total
        acc[2] += total * hat_in[s]
        acc[3] += total
        part[0:512, :] += dot(g, normed[s], 1, 0)
        return carry

    part[0:512, :] = jnp.zeros((512, 128), F32)
    lax.fori_loop(0, 8, inward, 0)
    norms = jnp.concatenate(
        [
            jnp.sum(acc[2], axis=0, keepdims=True),
            jnp.sum(acc[3], axis=0, keepdims=True),
            jnp.sum(acc[0].T, axis=0, keepdims=True),
            jnp.sum(acc[1].T, axis=0, keepdims=True),
            jnp.zeros((4, 128), F32),
        ],
        axis=0,
    )

    for which in range(2):
        a2_send[which * 16 : which * 16 + 16] = jnp.concatenate(
            [
                part[which * 256 : which * 256 + 256, :].reshape(16, 16, 128),
                part[512 + which * 128 : 640 + which * 128, :].reshape(16, 8, 128),
                jnp.broadcast_to(norms.reshape(1, 8, 128), (16, 8, 128)),
            ],
            axis=1,
        ).astype(BF16)
    slot = q * 16 + plane

    def plane_both(fn):
        each_plane(lambda dev, i: [fn((dev[0], dev[1] // 2 * 2 + core), core * 16 + i) for core in range(2)])
        fn(sibling, (1 - q) * 16 + plane)

    plane_both(lambda dev, i: remote(a2_send.at[i], a2_got.at[slot], A2, dev).start())
    a2_got[pl.ds(slot, 1)] = a2_send[pl.ds(slot, 1)]

    def last(s, carry):
        dhat = dn[s] * in_gain[...]
        hat = hat_in[s]
        mean_d = jnp.mean(dhat, axis=-1, keepdims=True)
        mean_dh = jnp.mean(dhat * hat, axis=-1, keepdims=True)
        cells(grad_pair, s, rstd_in[s] * (dhat - mean_d - hat * mean_dh))
        return carry

    lax.fori_loop(0, 4, last, 0)
    wait_slots(a2_got, 31, rsem.at[A2])
    a3_send[...] = jnp.sum(a2_got[...].astype(F32), axis=0).astype(BF16)
    each_z(lambda dev, i: remote(a3_send, a3_got.at[z], A3, dev).start())
    a3_got[pl.ds(z, 1)] = a3_send[...].reshape(1, 32, 128)
    lax.fori_loop(4, 8, last, 0)
    stores[1].start()
    wait_slots(a3_got, 7, rsem.at[A3])
    total = jnp.sum(a3_got[...].astype(F32), axis=0) * (1.0 / 512.0)
    g_norms[...] = total[24:32]
    a4_send[...] = total.astype(BF16)
    plane_both(lambda dev, i: remote(a4_send, a4_got.at[slot], A4, dev).start())
    a4_got[pl.ds(slot, 1)] = a4_send[...].reshape(1, 32, 128)
    wait_slots(a4_got, 31, rsem.at[A4])
    for which in range(2):
        piece = a4_got[which * 16 : which * 16 + 16].astype(F32)
        both = piece[:, 0:16].reshape(256, 128)
        g_weights[which * 2] = both[0:128].T
        g_weights[which * 2 + 1] = both[128:256].T
        g_weights[4 + which] = piece[:, 16:24].reshape(128, 128)

    stores[2].start()
    stores[3].start()
    wait_owners(send1, ssem.at[P1])
    wait_owners(send3, ssem.at[P3])

    @pl.when(own)
    def _():
        wait_slots(send2, 127, ssem.at[P2 + zl])
        wait_slots(send4, 127, ssem.at[P4 + zl])

    wait_slots(a2_send, 31, ssem.at[A2])
    wait_slots(a3_got, 7, ssem.at[A3])
    wait_slots(a4_got, 31, ssem.at[A4])
    for store in stores:
        store.wait()


def hand_out(update, grad_pair, g_weights, g_norms, *refs):
    outs, held, in_sems, sems = refs[:9], refs[9:13], refs[13], refs[14]
    loads = [
        pltpu.make_async_copy(a, b, in_sems.at[i])
        for i, (a, b) in enumerate(zip((update, grad_pair, g_weights, g_norms), held))
    ]
    sources = [held[0], held[1]] + [held[2].at[i] for i in range(6)] + [held[3].at[pl.ds(0, 4)]]
    copies = [pltpu.make_async_copy(a, b, sems.at[i]) for i, (a, b) in enumerate(zip(sources, outs))]
    for load in loads:
        load.start()
    for load, part in zip(loads, (copies[0:1], copies[1:2], copies[2:8], copies[8:9])):
        load.wait()
        for copy in part:
            copy.start()
    for copy in copies:
        copy.wait()


def scratch():
    def v(shape, kind=F32):
        return pltpu.VMEM(shape, kind)

    return [
        v((1024, 128)), v((1024, 128)), v((6, 128, 128)), v((8, 128)),
        v((1024, 128)), v((1024, 128)), v((16, 64), jnp.int32), v((1, 128)), v((1, 128)),
        v((128, 128), BF16), v((128, 128), BF16), v((128, 128), BF16), v((128, 128), BF16),
        v((1, 128)), v((1, 128)), v((128, 128), BF16), v((128, 128), BF16), v((8, 128)),
        v((128, 512), BF16), v((512, 128), BF16),
        v((8, 128, 128)), v((8, 128, 1)), v((8, 128, 128), BF16),
        v((4, 8, 128, 128)), v((2048, 128)),
        v((8, 128, 128)), v((8, 128, 128)), v((1024, 128), BF16),
        v((8, 128, 128)), v((8, 128, 128), BF16), v((1024, 128)),
        v((1024, 128), BF16), v((8, 128, 128)), v((8, 512, 128), BF16),
        v((2, 128, 128)), v((4, 128, 128)),
        v((64, 16, 128), BF16), v((64, 2, 16, 128), BF16), v((128, 2, 16, 128), BF16),
        v((512, 512), BF16), v((512, 512), BF16), v((512, 512), BF16),
        v((128, 16, 128), BF16), v((64, 16, 128), BF16),
        v((32, 16, 128), BF16), v((32, 16, 128), BF16),
        v((32, 16, 128), BF16), v((32, 16, 128), BF16),
        v((64, 16, 128), BF16), v((128, 16, 128), BF16),
        v((512, 512), BF16),
        v((128, 2, 16, 128), BF16), v((64, 2, 16, 128), BF16), v((64, 16, 128), BF16),
        v((768, 128)),
        v((32, 32, 128), BF16), v((32, 32, 128), BF16),
        v((32, 128), BF16), v((8, 32, 128), BF16),
        v((32, 128), BF16), v((32, 32, 128), BF16),
        pltpu.SemaphoreType.DMA((13,)),
        pltpu.SemaphoreType.DMA((4,)),
        pltpu.SemaphoreType.DMA((17,)),
        pltpu.SemaphoreType.DMA((17,)),
        pltpu.SemaphoreType.REGULAR,
    ]


def per_device(
    pair, pair_mask, cotangent, in_gain, in_bias, left_weight, left_gate_weight, right_weight, right_gate_weight,
    out_gain, out_bias, output_weight, output_gate_weight,
):
    hbm = pl.BlockSpec(memory_space=pl.ANY)
    square = jax.ShapeDtypeStruct((128, 128), F32)
    cells = jax.ShapeDtypeStruct((1024, 128), F32)
    found = pl.pallas_call(
        kernel,
        out_shape=(cells, cells, jax.ShapeDtypeStruct((6, 128, 128), F32), jax.ShapeDtypeStruct((8, 128), F32)),
        in_specs=[hbm] * 13,
        out_specs=(hbm,) * 4,
        scratch_shapes=scratch(),
        name="triangle",
        compiler_params=pltpu.CompilerParams(
            collective_id=1, has_side_effects=True, vmem_limit_bytes=60 * 1024 * 1024
        ),
    )(
        pair.reshape(1024, 128), cotangent.reshape(1024, 128), pair_mask.T, in_gain.reshape(1, 128), in_bias.reshape(1, 128),
        left_weight, left_gate_weight, right_weight, right_gate_weight,
        out_gain.reshape(1, 128), out_bias.reshape(1, 128), output_weight, output_gate_weight,
    )
    outs = pl.pallas_call(
        hand_out,
        out_shape=(cells, cells) + (square,) * 6 + (jax.ShapeDtypeStruct((4, 128), F32),),
        in_specs=[hbm] * 4,
        out_specs=(hbm,) * 9,
        scratch_shapes=[
            pltpu.VMEM((1024, 128), F32),
            pltpu.VMEM((1024, 128), F32),
            pltpu.VMEM((6, 128, 128), F32),
            pltpu.VMEM((8, 128), F32),
            pltpu.SemaphoreType.DMA((4,)),
            pltpu.SemaphoreType.DMA((9,)),
        ],
        name="hand_out",
        compiler_params=pltpu.CompilerParams(vmem_limit_bytes=60 * 1024 * 1024),
    )(*found)
    return (outs[0].reshape(64, 16, 128), outs[1].reshape(64, 16, 128)) + tuple(outs[2:])


def solution(mesh):
    cell, copied = P("row", "col", None), P()
    return jax.shard_map(
        per_device,
        mesh=mesh,
        in_specs=(cell, P("row", "col"), cell) + (copied,) * 10,
        out_specs=(cell, cell) + (copied,) * 7,
        check_vma=False,
    )
```

```python
import functools

import jax
import jax.numpy as jnp
from jax import lax
from jax.experimental import pallas as pl
from jax.experimental.pallas import tpu as pltpu
from jax.sharding import PartitionSpec as P

EPS = 1e-05
MESH = pl.DeviceIdType.MESH
F32, BF16 = jnp.float32, jnp.bfloat16
X1, X1B, P1, P2, P2B, X2, X2B, P3, X3, X3B, P4, P4B, X4, X4B, A2, A3, A4 = range(17)


def dot(a, b, ca, cb):
    return lax.dot_general(a, b, (((ca,), (cb,)), ((), ())), preferred_element_type=F32)


def swap_halves(a, b):
    low = lax.broadcasted_iota(jnp.int32, a.shape, 1) < 64
    return jnp.where(low, a, pltpu.roll(b, 64, 1)), jnp.where(low, pltpu.roll(a, 64, 1), b)


def kernel(
    pair_in, cot_in, mask_in, gi_in, bi_in, wl_in, wlg_in, wr_in, wrg_in, go_in, bo_in, wo_in, wog_in,
    update_out, grad_pair_out, pieces_out, g_norms_out,
    update, grad_pair, g_norms, xin, cin, pair_mask, in_gain, in_bias, wl, wlg, wr, wrg, out_gain, out_bias, wo, wog, mask, wcat, wcat_t, hat_in, rstd_in, normed, vs, stage, gate, slope, d_out, d_tn, tri_n, tri_f, d_gate, dn, dx,
    cols, acc, give1, send1, got1, lk, rk, rk_t, send2, got2, give2, take2, give3, take3, send3, got3, dt,
    send4, got4, take4, part, a2_send, a2_got, a3_send, a3_got, a4_send, out_norms,
    in_sems, out_sems, ssem, rsem, ready,
):
    row, col = lax.axis_index("row"), lax.axis_index("col")
    cc, q = col // 2, col % 2
    x, zl, zh, y = row // 2, row % 2, cc // 4, cc % 4
    z = zh * 2 + zl
    me = row * 16 + cc
    own = row // 4 == q
    not_own = jnp.logical_not(own)
    chan = zl * 32 + x % 2 * 16 + cc
    plane = x * 4 + y
    sibling = (row, cc * 2 + 1 - q)

    def remote(src, dst, k, dev):
        return pltpu.make_async_remote_copy(
            src_ref=src, dst_ref=dst, send_sem=ssem.at[k], recv_sem=rsem.at[k], device_id=dev, device_id_type=MESH
        )

    def wait_slots(buf, n, sem):
        pltpu.make_async_copy(buf.at[pl.ds(0, n)], buf.at[pl.ds(0, n)], sem).wait()

    far = {0: 2, 1: 1, 2: 3, 3: 0}
    offsets = sorted(((dx, dy) for dx in range(4) for dy in range(4)), key=lambda o: -min(o[0], 4 - o[0]) - min(o[1], 4 - o[1]))
    xs, ys = [(x + d) % 4 for d in range(4)], [(y + d) % 4 for d in range(4)]

    def ring(t):
        return (z + 4 + (1 - 2 * (t % 2)) * ((t + 1) // 2)) % 8

    def at_chip(px, py, pz, fn, index=None):
        prow, pcc = px * 2 + pz % 2, pz // 2 * 4 + py
        fn((prow, pcc * 2 + q), prow * 16 + pcc if index is None else index)

    def by_x(block):
        def step(t, carry):
            block((x + 2 + (1 - 2 * (t % 2)) * ((t + 1) // 2)) % 4)
            return carry

        lax.fori_loop(0, 4, step, 0)

    def send_half(half, fn):
        sides = (q * 2 + (x + 1) % 2, q * 2 + x % 2)
        targets = [(side, ys[far[d]]) for d in range(4) for side in sides]

        def step(t, carry):
            pz = (z + 4 + (1 - 2 * (t % 2)) * ((t + 1) // 2) * 2 + (z + half) % 2) % 8
            for px, py in targets:
                at_chip(px, py, pz, lambda dev, g: fn(dev, half * 32 + px % 2 * 16 + g % 16))
            return carry

        lax.fori_loop(0, 3, step, 0)
        pz = (z + (z + half) % 2) % 8
        for px, py in targets[:-1]:
            at_chip(px, py, pz, lambda dev, g: fn(dev, half * 32 + px % 2 * 16 + g % 16))

        @pl.when(jnp.logical_or(not_own, zl != half))
        def _():
            px, py = targets[-1]
            at_chip(px, py, pz, lambda dev, g: fn(dev, half * 32 + px % 2 * 16 + g % 16))

    def send_x(px, fn):
        def step(t, carry):
            pz = ring(t)
            for d in range(4):
                at_chip(px, ys[far[d]], pz, fn)
            return carry

        lax.fori_loop(0, 7, step, 0)
        for d in range(3):
            at_chip(px, ys[far[d]], z, fn)

        @pl.when(px != x)
        def _():
            at_chip(px, y, z, fn)

    def each_plane(fn):
        for dx, dy in offsets[:-1]:
            at_chip(xs[dx], ys[dy], z, fn, xs[dx] * 4 + ys[dy])

    def each_z(fn):
        def step(t, carry):
            pz = ring(t)
            at_chip(x, y, pz, fn, pz)
            return carry

        lax.fori_loop(0, 7, step, 0)

    def wait_owners(buf, sem):
        @pl.when(own)
        def _():
            wait_slots(buf, 63, sem)

        @pl.when(not_own)
        def _():
            wait_slots(buf, 64, sem)

    def wait_half(buf, half, sem):
        mine_too = jnp.logical_and(own, zl == half)

        @pl.when(mine_too)
        def _():
            wait_slots(buf, 31, sem)

        @pl.when(jnp.logical_not(mine_too))
        def _():
            wait_slots(buf, 32, sem)

    def signal(sem, dev):
        pl.semaphore_signal(sem, inc=1, device_id=dev, device_id_type=MESH)

    def cells(ref, s, put=None):
        for h in range(4):
            p, par = h // 2, h % 2
            at = pl.ds(par * 16 + 2 * s + p, 32, stride=32)
            if put is not None:
                ref[at, :] = put[h * 32 : h * 32 + 32]
        if put is None:
            return jnp.concatenate(
                [ref[pl.ds(par * 16 + 2 * s + p, 32, stride=32), :] for p in range(2) for par in range(2)], axis=0
            )

    sources = (pair_in, wl_in, wlg_in, wr_in, wrg_in, mask_in, gi_in, bi_in, go_in, bo_in, wo_in, wog_in, cot_in)
    places = (xin, wl, wlg, wr, wrg, pair_mask, in_gain, in_bias, out_gain, out_bias, wo, wog, cin)
    loads = [pltpu.make_async_copy(a, b, in_sems.at[i]) for i, (a, b) in enumerate(zip(sources, places))]
    for load in loads:
        load.start()
    stores = [
        pltpu.make_async_copy(a, b, out_sems.at[i])
        for i, (a, b) in enumerate(
            ((update, update_out), (grad_pair, grad_pair_out), (a4_send, pieces_out.at[q * 16 + plane]), (g_norms, g_norms_out))
        )
    ]
    bar = pltpu.get_barrier_semaphore()
    signal(bar, sibling)
    each_z(lambda dev, i: signal(bar, dev))
    each_plane(lambda dev, i: signal(bar, dev))

    for load in (loads[0], loads[6], loads[7]):
        load.wait()

    def center(s, carry):
        v = cells(xin, s)
        middle = v - jnp.mean(v, axis=-1, keepdims=True)
        rstd = lax.rsqrt(jnp.mean(middle * middle, axis=-1, keepdims=True) + EPS)
        hat = middle * rstd
        hat_in[s] = hat
        rstd_in[s] = rstd
        normed[s] = (hat * in_gain[...] + in_bias[...]).astype(BF16)
        return carry

    lax.fori_loop(0, 8, center, 0)
    for load in loads[1:6] + loads[8:12]:
        load.wait()
    for i, w in enumerate((wl, wlg, wr, wrg)):
        turned = w[...].astype(F32).T.astype(BF16)
        for half in range(2):
            for core in range(2):
                to = half * 256 + i * 64 + core * 32
                wcat_t[to : to + 32, :] = turned[core * 64 + half * 32 : core * 64 + half * 32 + 32]
    flags = pair_mask[...].astype(F32)
    laid = jnp.zeros((8, 128), F32)
    for p in range(2):
        pick = lax.broadcasted_iota(jnp.int32, (8, 16), 1) == 2 * lax.broadcasted_iota(jnp.int32, (8, 16), 0) + p
        lane = lax.broadcasted_iota(jnp.int32, (64, 128), 1)
        place = jnp.logical_and(
            lane // 64 == p, lax.broadcasted_iota(jnp.int32, (64, 128), 0) == 2 * (lane % 32) + (lane % 64) // 32
        )
        laid += dot(dot(pick.astype(F32), flags, 1, 0), place.astype(F32), 1, 0)
    mask[...] = laid
    pl.semaphore_wait(bar, 23)
    each_plane(lambda dev, i: signal(ready, dev))

    def project(half):
        def step(s, carry):
            both = dot(wcat_t[half * 256 : half * 256 + 256, :], normed[s], 1, 1)
            m = mask[pl.ds(s, 1), :]
            for side in range(2):
                val = both[side * 128 : side * 128 + 64]
                sig = jax.nn.sigmoid(both[side * 128 + 64 : side * 128 + 128])
                value = sig * val * m
                for core in range(2):
                    start = core * 64 + half * 32
                    rows = slice(core * 32, core * 32 + 32)
                    vs[side * 2, s, pl.ds(start, 32), :] = val[rows]
                    vs[side * 2 + 1, s, pl.ds(start, 32), :] = sig[rows]
                    stage[pl.ds(start * 16 + side * 8 + s, 32, stride=16), :] = value[rows]
            return carry

        lax.fori_loop(0, 8, step, 0)
        to = pl.ds(half * 32, 32)
        theirs = pl.ds(pl.multiple_of((1 - q) * 1024 + half * 512, 512), 512)
        ours = pl.ds(pl.multiple_of(q * 1024 + half * 512, 512), 512)
        give1[to] = stage[theirs, :].reshape(32, 16, 128).astype(BF16)
        send1[to, pl.ds(q, 1)] = stage[ours, :].reshape(32, 1, 16, 128).astype(BF16)
        copy = remote(give1.at[pl.ds(half * 32, 32)], send1.at[pl.ds(half * 32, 32), q], (X1, X1B)[half], sibling)
        copy.start()
        return copy

    x1 = [project(0), project(1)]
    other = pl.multiple_of((1 - q) * 1024, 1024)
    mine = pl.multiple_of(q * 1024, 1024)
    pl.semaphore_wait(ready, 15)
    for half in range(2):
        x1[half].wait()
        send_half(half, lambda dev, c: remote(send1.at[c], got1.at[me], P1, dev).start())

    @pl.when(own)
    def _():
        got1[pl.ds(me, 1)] = send1[pl.ds(chan, 1)]

    @pl.when(own)
    def _():
        wait_slots(got1, 127, rsem.at[P1])
        for rp in range(4):
            a = got1[rp * 32 : rp * 32 + 16].astype(F32)
            b = got1[rp * 32 + 16 : rp * 32 + 32].astype(F32)
            for part_k, dst in ((0, lk), (8, rk)):
                lo, hi = swap_halves(
                    a[:, :, part_k : part_k + 8].reshape(256, 128), b[:, :, part_k : part_k + 8].reshape(256, 128)
                )
                dst[0:256, rp * 128 : rp * 128 + 128] = lo.astype(BF16)
                dst[256:512, rp * 128 : rp * 128 + 128] = hi.astype(BF16)
        rk_t[...] = rk[...].astype(F32).T.astype(BF16)

        def block(px):
            lanes = pl.ds(pl.multiple_of(px * 128, 128), 128)
            v = dot(rk_t[...], lk[:, lanes], 1, 0).reshape(8, 2, 32, 128)
            lo, hi = swap_halves(v[:, 0].reshape(256, 128), v[:, 1].reshape(256, 128))
            send2[pl.ds(px * 32, 16)] = lo.reshape(16, 16, 128).astype(BF16)
            send2[pl.ds(px * 32 + 16, 16)] = hi.reshape(16, 16, 128).astype(BF16)
            send_x(px, lambda dev, t: remote(send2.at[t], got2.at[chan], P2 + zl, dev).start())

        by_x(block)
        got2[pl.ds(chan, 1)] = send2[pl.ds(me, 1)]

    loads[12].wait()
    wcat[...] = jnp.concatenate([wl[...], wlg[...], wr[...], wrg[...]], axis=1)
    cols[0] = jnp.broadcast_to(out_gain[...], (128, 128)).T
    cols[1] = jnp.broadcast_to(out_bias[...], (128, 128)).T

    def gates(s, carry):
        n = normed[s]
        g = jax.nn.sigmoid(dot(n, wog[...], 1, 0))
        ct = cells(cin, s)
        do = (ct * g).astype(BF16)
        gate[s] = g
        slope[s] = ct * g * (1.0 - g)
        d_out[pl.ds(pl.multiple_of(s * 128, 128), 128), :] = do
        d_tn[s] = dot(wo[...], do, 1, 1)
        return carry

    lax.fori_loop(0, 8, gates, 0)

    first = q == 0
    x2 = []
    for half in range(2):
        wait_half(got2, half, rsem.at[(P2, P2B)[half]])
        tri = got2[half * 32 : half * 32 + 32].astype(F32)
        tri_lo, tri_hi = tri[:, 0:8], tri[:, 8:16]
        part2 = pl.ds(half * 16, 16)
        give2[part2] = jnp.where(first, tri_hi, tri_lo).reshape(16, 16, 128).astype(BF16)
        x2.append(remote(give2.at[part2], take2.at[part2], (X2, X2B)[half], sibling))
        x2[half].start()
        ours = pl.ds(pl.multiple_of(q * 512 + half * 256, 256), 256)
        stage[ours, :] = jnp.where(first, tri_lo, tri_hi).reshape(256, 128)
    for half in range(2):
        x2[half].wait()
        theirs = pl.ds(pl.multiple_of((1 - q) * 512 + half * 256, 256), 256)
        stage[theirs, :] = take2[half * 16 : half * 16 + 16].astype(F32).reshape(256, 128)
    acc[...] = jnp.zeros_like(acc)

    def triangle(s, carry):
        at = pl.ds(s, 128, stride=8)
        t = stage[at, :]
        center = t - jnp.mean(t, axis=0, keepdims=True)
        rstd = lax.rsqrt(jnp.mean(center * center, axis=0, keepdims=True) + EPS)
        hat = center * rstd
        tri_n[s] = (hat * cols[0] + cols[1]).astype(BF16)
        d = d_tn[s]
        dh = d * cols[0]
        mean_dh = jnp.mean(dh, axis=0, keepdims=True)
        mean_dhh = jnp.mean(dh * hat, axis=0, keepdims=True)
        tri_f[at, :] = rstd * (dh - mean_dh - hat * mean_dhh)
        acc[0] += d * hat
        acc[1] += d
        return carry

    lax.fori_loop(0, 8, triangle, 0)
    x3 = []
    for half in range(2):
        theirs = pl.ds(pl.multiple_of((1 - q) * 512 + half * 256, 256), 256)
        part3 = pl.ds(half * 16, 16)
        give3[part3] = tri_f[theirs, :].reshape(16, 16, 128).astype(BF16)
        x3.append(remote(give3.at[part3], take3.at[part3], (X3, X3B)[half], sibling))
        x3[half].start()
    for half in range(2):
        kept = tri_f[pl.ds(pl.multiple_of(q * 512 + half * 256, 256), 256), :].reshape(32, 8, 128)
        x3[half].wait()
        came = take3[pl.ds(half * 16, 16)].astype(F32).reshape(32, 8, 128)
        send3[pl.ds(half * 32, 32)] = jnp.concatenate(
            [jnp.where(first, kept, came), jnp.where(first, came, kept)], axis=1
        ).astype(BF16)
        send_half(half, lambda dev, c: remote(send3.at[c], got3.at[me], P3, dev).start())

    @pl.when(own)
    def _():
        got3[pl.ds(me, 1)] = send3[pl.ds(chan, 1)]

    @pl.when(own)
    def _():
        wait_slots(got3, 127, rsem.at[P3])
        for rp in range(4):
            a = got3[rp * 32 : rp * 32 + 16].astype(F32).reshape(256, 128)
            b = got3[rp * 32 + 16 : rp * 32 + 32].astype(F32).reshape(256, 128)
            lo, hi = swap_halves(a, b)
            dt[:, rp * 128 : rp * 128 + 128] = (
                jnp.concatenate([lo.reshape(8, 1, 32, 128), hi.reshape(8, 1, 32, 128)], axis=1)
                .reshape(512, 128)
                .astype(BF16)
            )

        def block(px):
            lanes = pl.ds(pl.multiple_of(px * 128, 128), 128)
            left = dot(rk[...], dt[:, lanes], 1, 0)
            right = dot(lk[...], dt[lanes, :], 1, 1)
            l_lo, l_hi = swap_halves(left[0:256], left[256:512])
            r_lo, r_hi = swap_halves(right[0:256], right[256:512])
            shape = (16, 2, 8, 128)
            send4[pl.ds(px * 32, 16)] = jnp.concatenate([l_lo.reshape(shape), r_lo.reshape(shape)], axis=2).astype(BF16)
            send4[pl.ds(px * 32 + 16, 16)] = jnp.concatenate(
                [l_hi.reshape(shape), r_hi.reshape(shape)], axis=2
            ).astype(BF16)
            send_x(px, lambda dev, t: remote(send4.at[t], got4.at[chan], P4 + zl, dev).start())

        by_x(block)
        got4[pl.ds(chan, 1)] = send4[pl.ds(me, 1)]

    def outputs(s, carry):
        at = pl.ds(pl.multiple_of(s * 128, 128), 128)
        proj = dot(tri_n[s], wo[...], 0, 0)
        cells(update, s, gate[s] * proj)
        dg = (slope[s] * proj).astype(BF16)
        d_gate[at, :] = dg
        dn[s] = dot(dg, wog[...], 1, 1)
        part[512:640, :] += dot(tri_n[s], d_out[at, :], 1, 0)
        part[640:768, :] += dot(normed[s], dg, 0, 0)
        return carry

    part[512:768, :] = jnp.zeros((256, 128), F32)
    lax.fori_loop(0, 8, outputs, 0)
    stores[0].start()
    for i in range(2):
        out_norms[i : i + 1, :] = jnp.sum(acc[i].T, axis=0, keepdims=True)

    x4 = []
    for half in range(2):
        wait_half(got4, half, rsem.at[(P4, P4B)[half]])
        part4 = pl.ds(half * 32, 32)
        x4.append(remote(got4.at[part4, 1 - q], take4.at[part4], (X4, X4B)[half], sibling))
        x4[half].start()
        ours = pl.ds(pl.multiple_of(q * 1024 + half * 512, 512), 512)
        stage[ours, :] = got4[part4, pl.ds(q, 1)].astype(F32).reshape(512, 128)
    for half in range(2):
        x4[half].wait()
        theirs = pl.ds(pl.multiple_of((1 - q) * 1024 + half * 512, 512), 512)
        stage[theirs, :] = take4[half * 32 : half * 32 + 32].astype(F32).reshape(512, 128)
    def inward(s, carry):
        m = mask[pl.ds(s, 1), :]
        parts = []
        for side in range(2):
            d = stage[pl.ds(side * 8 + s, 128, stride=16), :] * m
            val, sig = vs[side * 2, s], vs[side * 2 + 1, s]
            parts.append((d * sig).astype(BF16))
            parts.append((d * val * sig * (1.0 - sig)).astype(BF16))
        g = jnp.concatenate(parts, axis=0)
        dx[s] = g
        total = dn[s] + dot(g, wcat[...], 0, 1)
        dn[s] = total
        acc[2] += total * hat_in[s]
        acc[3] += total
        part[0:512, :] += dot(g, normed[s], 1, 0)
        return carry

    part[0:512, :] = jnp.zeros((512, 128), F32)
    lax.fori_loop(0, 8, inward, 0)
    norms = jnp.concatenate(
        [
            jnp.sum(acc[2], axis=0, keepdims=True),
            jnp.sum(acc[3], axis=0, keepdims=True),
            out_norms[...],
            jnp.zeros((4, 128), F32),
        ],
        axis=0,
    )

    for which in range(2):
        a2_send[which * 16 : which * 16 + 16] = jnp.concatenate(
            [
                part[which * 256 : which * 256 + 256, :].reshape(16, 16, 128),
                part[512 + which * 128 : 640 + which * 128, :].reshape(16, 8, 128),
                jnp.broadcast_to(norms.reshape(1, 8, 128), (16, 8, 128)),
            ],
            axis=1,
        ).astype(BF16)
    slot = q * 16 + plane

    def plane_both(fn):
        each_plane(lambda dev, i: [fn((dev[0], dev[1] // 2 * 2 + core), core * 16 + i) for core in range(2)])
        fn(sibling, (1 - q) * 16 + plane)

    plane_both(lambda dev, i: remote(a2_send.at[i], a2_got.at[slot], A2, dev).start())
    a2_got[pl.ds(slot, 1)] = a2_send[pl.ds(slot, 1)]

    def last(s, carry):
        dhat = dn[s] * in_gain[...]
        hat = hat_in[s]
        mean_d = jnp.mean(dhat, axis=-1, keepdims=True)
        mean_dh = jnp.mean(dhat * hat, axis=-1, keepdims=True)
        cells(grad_pair, s, rstd_in[s] * (dhat - mean_d - hat * mean_dh))
        return carry

    lax.fori_loop(0, 4, last, 0)
    wait_slots(a2_got, 31, rsem.at[A2])
    a3_send[...] = jnp.sum(a2_got[...].astype(F32), axis=0).astype(BF16)
    each_z(lambda dev, i: remote(a3_send, a3_got.at[z], A3, dev).start())
    a3_got[pl.ds(z, 1)] = a3_send[...].reshape(1, 32, 128)
    lax.fori_loop(4, 8, last, 0)
    stores[1].start()
    wait_slots(a3_got, 7, rsem.at[A3])
    total = jnp.sum(a3_got[...].astype(F32), axis=0) * (1.0 / 512.0)
    g_norms[...] = total[24:32]
    a4_send[...] = total.astype(BF16)
    plane_both(lambda dev, i: remote(a4_send, pieces_out.at[slot], A4, dev).start())
    stores[2].start()
    stores[3].start()
    wait_slots(pieces_out, 31, rsem.at[A4])

    wait_owners(send1, ssem.at[P1])
    wait_owners(send3, ssem.at[P3])

    @pl.when(own)
    def _():
        wait_slots(send2, 127, ssem.at[P2 + zl])
        wait_slots(send4, 127, ssem.at[P4 + zl])

    wait_slots(a2_send, 31, ssem.at[A2])
    wait_slots(a3_got, 7, ssem.at[A3])
    wait_slots(pieces_out, 31, ssem.at[A4])
    for store in stores:
        store.wait()


def hand_out(update, grad_pair, pieces, g_norms, *refs):
    outs, held, weights, in_sems, sems = refs[:9], refs[9:13], refs[13], refs[14], refs[15]
    loads = [
        pltpu.make_async_copy(a, b, in_sems.at[i])
        for i, (a, b) in enumerate(zip((pieces, update, grad_pair, g_norms), held))
    ]
    sources = [held[1], held[2]] + [weights.at[i] for i in range(6)] + [held[3].at[pl.ds(0, 4)]]
    copies = [pltpu.make_async_copy(a, b, sems.at[i]) for i, (a, b) in enumerate(zip(sources, outs))]
    for load in loads:
        load.start()
    loads[0].wait()
    for which in range(2):
        piece = held[0][which * 16 : which * 16 + 16].astype(F32)
        both = piece[:, 0:16].reshape(256, 128)
        weights[which * 2] = both[0:128].T
        weights[which * 2 + 1] = both[128:256].T
        weights[4 + which] = piece[:, 16:24].reshape(128, 128)
        for i in (which * 2, which * 2 + 1, 4 + which):
            copies[2 + i].start()
    for load, copy in zip(loads[1:], (copies[0], copies[1], copies[8])):
        load.wait()
        copy.start()
    for copy in copies:
        copy.wait()


def scratch():
    def v(shape, kind=F32):
        return pltpu.VMEM(shape, kind)

    return [
        v((1024, 128)), v((1024, 128)), v((8, 128)),
        v((1024, 128)), v((1024, 128)), v((16, 64), jnp.int32), v((1, 128)), v((1, 128)),
        v((128, 128), BF16), v((128, 128), BF16), v((128, 128), BF16), v((128, 128), BF16),
        v((1, 128)), v((1, 128)), v((128, 128), BF16), v((128, 128), BF16), v((8, 128)),
        v((128, 512), BF16), v((512, 128), BF16),
        v((8, 128, 128)), v((8, 128, 1)), v((8, 128, 128), BF16),
        v((4, 8, 128, 128)), v((2048, 128)),
        v((8, 128, 128)), v((8, 128, 128)), v((1024, 128), BF16),
        v((8, 128, 128)), v((8, 128, 128), BF16), v((1024, 128)),
        v((1024, 128), BF16), v((8, 128, 128)), v((8, 512, 128), BF16),
        v((2, 128, 128)), v((4, 128, 128)),
        v((64, 16, 128), BF16), v((64, 2, 16, 128), BF16), v((128, 2, 16, 128), BF16),
        v((512, 512), BF16), v((512, 512), BF16), v((512, 512), BF16),
        v((128, 16, 128), BF16), v((64, 16, 128), BF16),
        v((32, 16, 128), BF16), v((32, 16, 128), BF16),
        v((32, 16, 128), BF16), v((32, 16, 128), BF16),
        v((64, 16, 128), BF16), v((128, 16, 128), BF16),
        v((512, 512), BF16),
        v((128, 2, 16, 128), BF16), v((64, 2, 16, 128), BF16), v((64, 16, 128), BF16),
        v((768, 128)),
        v((32, 32, 128), BF16), v((32, 32, 128), BF16),
        v((32, 128), BF16), v((8, 32, 128), BF16),
        v((32, 128), BF16), v((2, 128)),
        pltpu.SemaphoreType.DMA((13,)),
        pltpu.SemaphoreType.DMA((4,)),
        pltpu.SemaphoreType.DMA((17,)),
        pltpu.SemaphoreType.DMA((17,)),
        pltpu.SemaphoreType.REGULAR,
    ]


def per_device(
    pair, pair_mask, cotangent, in_gain, in_bias, left_weight, left_gate_weight, right_weight, right_gate_weight,
    out_gain, out_bias, output_weight, output_gate_weight,
):
    hbm = pl.BlockSpec(memory_space=pl.ANY)
    square = jax.ShapeDtypeStruct((128, 128), F32)
    cells = jax.ShapeDtypeStruct((1024, 128), F32)
    found = pl.pallas_call(
        kernel,
        out_shape=(cells, cells, jax.ShapeDtypeStruct((32, 32, 128), BF16), jax.ShapeDtypeStruct((8, 128), F32)),
        in_specs=[hbm] * 13,
        out_specs=(hbm,) * 4,
        scratch_shapes=scratch(),
        name="triangle",
        compiler_params=pltpu.CompilerParams(
            collective_id=1, has_side_effects=True, vmem_limit_bytes=60 * 1024 * 1024
        ),
    )(
        pair.reshape(1024, 128), cotangent.reshape(1024, 128), pair_mask.T, in_gain.reshape(1, 128), in_bias.reshape(1, 128),
        left_weight, left_gate_weight, right_weight, right_gate_weight,
        out_gain.reshape(1, 128), out_bias.reshape(1, 128), output_weight, output_gate_weight,
    )
    outs = pl.pallas_call(
        hand_out,
        out_shape=(cells, cells) + (square,) * 6 + (jax.ShapeDtypeStruct((4, 128), F32),),
        in_specs=[hbm] * 4,
        out_specs=(hbm,) * 9,
        scratch_shapes=[
            pltpu.VMEM((32, 32, 128), BF16),
            pltpu.VMEM((1024, 128), F32),
            pltpu.VMEM((1024, 128), F32),
            pltpu.VMEM((8, 128), F32),
            pltpu.VMEM((6, 128, 128), F32),
            pltpu.SemaphoreType.DMA((4,)),
            pltpu.SemaphoreType.DMA((9,)),
        ],
        name="hand_out",
        compiler_params=pltpu.CompilerParams(vmem_limit_bytes=60 * 1024 * 1024),
    )(*found)
    return (outs[0].reshape(64, 16, 128), outs[1].reshape(64, 16, 128)) + tuple(outs[2:])


def solution(mesh):
    cell, copied = P("row", "col", None), P()
    return jax.shard_map(
        per_device,
        mesh=mesh,
        in_specs=(cell, P("row", "col"), cell) + (copied,) * 10,
        out_specs=(cell, cell) + (copied,) * 7,
        check_vma=False,
    )
```

```python
import functools

import jax
import jax.numpy as jnp
from jax import lax
from jax.experimental import pallas as pl
from jax.experimental.pallas import tpu as pltpu
from jax.sharding import PartitionSpec as P

EPS = 1e-05
MESH = pl.DeviceIdType.MESH
F32, BF16 = jnp.float32, jnp.bfloat16
X1, X1B, P1, P2, P2B, X2, X2B, P3, X3, X3B, P4, P4B, X4, X4B, A2, A3, A4 = range(17)


def dot(a, b, ca, cb):
    return lax.dot_general(a, b, (((ca,), (cb,)), ((), ())), preferred_element_type=F32)


def swap_halves(a, b):
    low = lax.broadcasted_iota(jnp.int32, a.shape, 1) < 64
    return jnp.where(low, a, pltpu.roll(b, 64, 1)), jnp.where(low, pltpu.roll(a, 64, 1), b)


def kernel(
    pair_in, cot_in, mask_in, gi_in, bi_in, wl_in, wlg_in, wr_in, wrg_in, go_in, bo_in, wo_in, wog_in,
    update_out, grad_pair_out, pieces_out, g_norms_out,
    update, grad_pair, g_norms, xin, cin, pair_mask, in_gain, in_bias, wl, wlg, wr, wrg, out_gain, out_bias, wo, wog, mask, wcat, wcat_t, hat_in, rstd_in, normed, vs, stage, gate, slope, d_out, d_tn, tri_n, tri_f, d_gate, dn, dx,
    cols, acc, give1, send1, got1, lk, rk, rk_t, send2, got2, give2, take2, give3, take3, send3, got3, dt,
    send4, got4, take4, part, a2_send, a2_got, a3_send, a3_got, a4_send, out_norms,
    in_sems, out_sems, ssem, rsem, ready,
):
    row, col = lax.axis_index("row"), lax.axis_index("col")
    cc, q = col // 2, col % 2
    x, zl, zh, y = row // 2, row % 2, cc // 4, cc % 4
    z = zh * 2 + zl
    me = row * 16 + cc
    own = row // 4 == q
    not_own = jnp.logical_not(own)
    chan = zl * 32 + x % 2 * 16 + cc
    plane = x * 4 + y
    sibling = (row, cc * 2 + 1 - q)

    def remote(src, dst, k, dev):
        return pltpu.make_async_remote_copy(
            src_ref=src, dst_ref=dst, send_sem=ssem.at[k], recv_sem=rsem.at[k], device_id=dev, device_id_type=MESH
        )

    def wait_slots(buf, n, sem):
        pltpu.make_async_copy(buf.at[pl.ds(0, n)], buf.at[pl.ds(0, n)], sem).wait()

    far = {0: 2, 1: 1, 2: 3, 3: 0}
    offsets = sorted(((dx, dy) for dx in range(4) for dy in range(4)), key=lambda o: -min(o[0], 4 - o[0]) - min(o[1], 4 - o[1]))
    xs, ys = [(x + d) % 4 for d in range(4)], [(y + d) % 4 for d in range(4)]

    def ring(t):
        return (z + 4 + (1 - 2 * (t % 2)) * ((t + 1) // 2)) % 8

    def at_chip(px, py, pz, fn, index=None):
        prow, pcc = px * 2 + pz % 2, pz // 2 * 4 + py
        fn((prow, pcc * 2 + q), prow * 16 + pcc if index is None else index)

    def by_x(block):
        def step(t, carry):
            block((x + 2 + (1 - 2 * (t % 2)) * ((t + 1) // 2)) % 4)
            return carry

        lax.fori_loop(0, 4, step, 0)

    def send_half(half, fn):
        sides = (q * 2 + (x + 1) % 2, q * 2 + x % 2)
        targets = [(side, ys[far[d]]) for d in range(4) for side in sides]

        def step(t, carry):
            pz = (z + 4 + (1 - 2 * (t % 2)) * ((t + 1) // 2) * 2 + (z + half) % 2) % 8
            for px, py in targets:
                at_chip(px, py, pz, lambda dev, g: fn(dev, half * 32 + px % 2 * 16 + g % 16))
            return carry

        lax.fori_loop(0, 3, step, 0)
        pz = (z + (z + half) % 2) % 8
        for px, py in targets[:-1]:
            at_chip(px, py, pz, lambda dev, g: fn(dev, half * 32 + px % 2 * 16 + g % 16))

        @pl.when(jnp.logical_or(not_own, zl != half))
        def _():
            px, py = targets[-1]
            at_chip(px, py, pz, lambda dev, g: fn(dev, half * 32 + px % 2 * 16 + g % 16))

    def send_x(px, fn):
        def step(t, carry):
            pz = ring(t)
            for d in range(4):
                at_chip(px, ys[far[d]], pz, fn)
            return carry

        lax.fori_loop(0, 7, step, 0)
        for d in range(3):
            at_chip(px, ys[far[d]], z, fn)

        @pl.when(px != x)
        def _():
            at_chip(px, y, z, fn)

    def each_plane(fn):
        for dx, dy in offsets[:-1]:
            at_chip(xs[dx], ys[dy], z, fn, xs[dx] * 4 + ys[dy])

    def each_z(fn):
        def step(t, carry):
            pz = ring(t)
            at_chip(x, y, pz, fn, pz)
            return carry

        lax.fori_loop(0, 7, step, 0)

    def wait_owners(buf, sem):
        @pl.when(own)
        def _():
            wait_slots(buf, 63, sem)

        @pl.when(not_own)
        def _():
            wait_slots(buf, 64, sem)

    def wait_half(buf, half, sem):
        mine_too = jnp.logical_and(own, zl == half)

        @pl.when(mine_too)
        def _():
            wait_slots(buf, 31, sem)

        @pl.when(jnp.logical_not(mine_too))
        def _():
            wait_slots(buf, 32, sem)

    def signal(sem, dev):
        pl.semaphore_signal(sem, inc=1, device_id=dev, device_id_type=MESH)

    def cells(ref, s, put=None):
        for h in range(4):
            p, par = h // 2, h % 2
            at = pl.ds(par * 16 + 2 * s + p, 32, stride=32)
            if put is not None:
                ref[at, :] = put[h * 32 : h * 32 + 32]
        if put is None:
            return jnp.concatenate(
                [ref[pl.ds(par * 16 + 2 * s + p, 32, stride=32), :] for p in range(2) for par in range(2)], axis=0
            )

    sources = (pair_in, wl_in, wlg_in, wr_in, wrg_in, mask_in, gi_in, bi_in, go_in, bo_in, wo_in, wog_in, cot_in)
    places = (xin, wl, wlg, wr, wrg, pair_mask, in_gain, in_bias, out_gain, out_bias, wo, wog, cin)
    loads = [pltpu.make_async_copy(a, b, in_sems.at[i]) for i, (a, b) in enumerate(zip(sources, places))]
    for load in loads:
        load.start()
    stores = [
        pltpu.make_async_copy(a, b, out_sems.at[i])
        for i, (a, b) in enumerate(
            ((update, update_out), (grad_pair, grad_pair_out), (a4_send, pieces_out.at[q * 16 + plane]), (g_norms, g_norms_out))
        )
    ]
    bar = pltpu.get_barrier_semaphore()
    signal(bar, sibling)
    each_z(lambda dev, i: signal(bar, dev))
    each_plane(lambda dev, i: signal(bar, dev))

    for load in (loads[0], loads[6], loads[7]):
        load.wait()

    def center(s, carry):
        v = cells(xin, s)
        middle = v - jnp.mean(v, axis=-1, keepdims=True)
        rstd = lax.rsqrt(jnp.mean(middle * middle, axis=-1, keepdims=True) + EPS)
        hat = middle * rstd
        hat_in[s] = hat
        rstd_in[s] = rstd
        normed[s] = (hat * in_gain[...] + in_bias[...]).astype(BF16)
        return carry

    lax.fori_loop(0, 8, center, 0)
    for load in loads[1:6] + loads[8:12]:
        load.wait()
    for i, w in enumerate((wl, wlg, wr, wrg)):
        turned = w[...].astype(F32).T.astype(BF16)
        for half in range(2):
            for core in range(2):
                to = half * 256 + i * 64 + core * 32
                wcat_t[to : to + 32, :] = turned[core * 64 + half * 32 : core * 64 + half * 32 + 32]
    flags = pair_mask[...].astype(F32)
    laid = jnp.zeros((8, 128), F32)
    for p in range(2):
        pick = lax.broadcasted_iota(jnp.int32, (8, 16), 1) == 2 * lax.broadcasted_iota(jnp.int32, (8, 16), 0) + p
        lane = lax.broadcasted_iota(jnp.int32, (64, 128), 1)
        place = jnp.logical_and(
            lane // 64 == p, lax.broadcasted_iota(jnp.int32, (64, 128), 0) == 2 * (lane % 32) + (lane % 64) // 32
        )
        laid += dot(dot(pick.astype(F32), flags, 1, 0), place.astype(F32), 1, 0)
    mask[...] = laid
    pl.semaphore_wait(bar, 23)
    each_plane(lambda dev, i: signal(ready, dev))

    def project(half):
        def step(s, carry):
            both = dot(wcat_t[half * 256 : half * 256 + 256, :], normed[s], 1, 1)
            m = mask[pl.ds(s, 1), :]
            for side in range(2):
                val = both[side * 128 : side * 128 + 64]
                sig = jax.nn.sigmoid(both[side * 128 + 64 : side * 128 + 128])
                value = sig * val * m
                for core in range(2):
                    start = core * 64 + half * 32
                    rows = slice(core * 32, core * 32 + 32)
                    vs[side * 2, s, pl.ds(start, 32), :] = val[rows]
                    vs[side * 2 + 1, s, pl.ds(start, 32), :] = sig[rows]
                    stage[pl.ds(start * 16 + side * 8 + s, 32, stride=16), :] = value[rows]
            return carry

        lax.fori_loop(0, 8, step, 0)
        to = pl.ds(half * 32, 32)
        theirs = pl.ds(pl.multiple_of((1 - q) * 1024 + half * 512, 512), 512)
        ours = pl.ds(pl.multiple_of(q * 1024 + half * 512, 512), 512)
        give1[to] = stage[theirs, :].reshape(32, 16, 128).astype(BF16)
        send1[to, pl.ds(q, 1)] = stage[ours, :].reshape(32, 1, 16, 128).astype(BF16)
        copy = remote(give1.at[pl.ds(half * 32, 32)], send1.at[pl.ds(half * 32, 32), q], (X1, X1B)[half], sibling)
        copy.start()
        return copy

    x1 = [project(0), project(1)]
    other = pl.multiple_of((1 - q) * 1024, 1024)
    mine = pl.multiple_of(q * 1024, 1024)
    pl.semaphore_wait(ready, 15)
    for half in range(2):
        x1[half].wait()
        send_half(half, lambda dev, c: remote(send1.at[c], got1.at[me], P1, dev).start())

    @pl.when(own)
    def _():
        got1[pl.ds(me, 1)] = send1[pl.ds(chan, 1)]

    @pl.when(own)
    def _():
        wait_slots(got1, 127, rsem.at[P1])
        for rp in range(4):
            a = got1[rp * 32 : rp * 32 + 16].astype(F32)
            b = got1[rp * 32 + 16 : rp * 32 + 32].astype(F32)
            for part_k, dst in ((0, lk), (8, rk)):
                lo, hi = swap_halves(
                    a[:, :, part_k : part_k + 8].reshape(256, 128), b[:, :, part_k : part_k + 8].reshape(256, 128)
                )
                dst[0:256, rp * 128 : rp * 128 + 128] = lo.astype(BF16)
                dst[256:512, rp * 128 : rp * 128 + 128] = hi.astype(BF16)
        rk_t[...] = rk[...].astype(F32).T.astype(BF16)

        def block(px):
            lanes = pl.ds(pl.multiple_of(px * 128, 128), 128)
            v = dot(rk_t[...], lk[:, lanes], 1, 0).reshape(8, 2, 32, 128)
            lo, hi = swap_halves(v[:, 0].reshape(256, 128), v[:, 1].reshape(256, 128))
            send2[pl.ds(px * 32, 16)] = lo.reshape(16, 16, 128).astype(BF16)
            send2[pl.ds(px * 32 + 16, 16)] = hi.reshape(16, 16, 128).astype(BF16)
            send_x(px, lambda dev, t: remote(send2.at[t], got2.at[chan], P2 + zl, dev).start())

        by_x(block)
        got2[pl.ds(chan, 1)] = send2[pl.ds(me, 1)]

    loads[12].wait()
    wcat[...] = jnp.concatenate([wl[...], wlg[...], wr[...], wrg[...]], axis=1)
    cols[0] = jnp.broadcast_to(out_gain[...], (128, 128)).T
    cols[1] = jnp.broadcast_to(out_bias[...], (128, 128)).T

    def gates(s, carry):
        n = normed[s]
        g = jax.nn.sigmoid(dot(n, wog[...], 1, 0))
        ct = cells(cin, s)
        do = (ct * g).astype(BF16)
        gate[s] = g
        slope[s] = ct * g * (1.0 - g)
        d_out[pl.ds(pl.multiple_of(s * 128, 128), 128), :] = do
        d_tn[s] = dot(wo[...], do, 1, 1)
        return carry

    lax.fori_loop(0, 8, gates, 0)

    first = q == 0
    x2 = []
    for half in range(2):
        wait_half(got2, half, rsem.at[(P2, P2B)[half]])
        tri = got2[half * 32 : half * 32 + 32].astype(F32)
        tri_lo, tri_hi = tri[:, 0:8], tri[:, 8:16]
        part2 = pl.ds(half * 16, 16)
        give2[part2] = jnp.where(first, tri_hi, tri_lo).reshape(16, 16, 128).astype(BF16)
        x2.append(remote(give2.at[part2], take2.at[part2], (X2, X2B)[half], sibling))
        x2[half].start()
        ours = pl.ds(pl.multiple_of(q * 512 + half * 256, 256), 256)
        stage[ours, :] = jnp.where(first, tri_lo, tri_hi).reshape(256, 128)
    for half in range(2):
        x2[half].wait()
        theirs = pl.ds(pl.multiple_of((1 - q) * 512 + half * 256, 256), 256)
        stage[theirs, :] = take2[half * 16 : half * 16 + 16].astype(F32).reshape(256, 128)
    acc[...] = jnp.zeros_like(acc)

    def triangle(s, carry):
        at = pl.ds(s, 128, stride=8)
        t = stage[at, :]
        center = t - jnp.mean(t, axis=0, keepdims=True)
        rstd = lax.rsqrt(jnp.mean(center * center, axis=0, keepdims=True) + EPS)
        hat = center * rstd
        tri_n[s] = (hat * cols[0] + cols[1]).astype(BF16)
        d = d_tn[s]
        dh = d * cols[0]
        mean_dh = jnp.mean(dh, axis=0, keepdims=True)
        mean_dhh = jnp.mean(dh * hat, axis=0, keepdims=True)
        tri_f[at, :] = rstd * (dh - mean_dh - hat * mean_dhh)
        acc[0] += d * hat
        acc[1] += d
        return carry

    lax.fori_loop(0, 8, triangle, 0)
    x3 = []
    for half in range(2):
        theirs = pl.ds(pl.multiple_of((1 - q) * 512 + half * 256, 256), 256)
        part3 = pl.ds(half * 16, 16)
        give3[part3] = tri_f[theirs, :].reshape(16, 16, 128).astype(BF16)
        x3.append(remote(give3.at[part3], take3.at[part3], (X3, X3B)[half], sibling))
        x3[half].start()
    for half in range(2):
        kept = tri_f[pl.ds(pl.multiple_of(q * 512 + half * 256, 256), 256), :].reshape(32, 8, 128)
        x3[half].wait()
        came = take3[pl.ds(half * 16, 16)].astype(F32).reshape(32, 8, 128)
        send3[pl.ds(half * 32, 32)] = jnp.concatenate(
            [jnp.where(first, kept, came), jnp.where(first, came, kept)], axis=1
        ).astype(BF16)
        send_half(half, lambda dev, c: remote(send3.at[c], got3.at[me], P3, dev).start())

    @pl.when(own)
    def _():
        got3[pl.ds(me, 1)] = send3[pl.ds(chan, 1)]

    @pl.when(own)
    def _():
        wait_slots(got3, 127, rsem.at[P3])
        for rp in range(4):
            a = got3[rp * 32 : rp * 32 + 16].astype(F32).reshape(256, 128)
            b = got3[rp * 32 + 16 : rp * 32 + 32].astype(F32).reshape(256, 128)
            lo, hi = swap_halves(a, b)
            dt[:, rp * 128 : rp * 128 + 128] = (
                jnp.concatenate([lo.reshape(8, 1, 32, 128), hi.reshape(8, 1, 32, 128)], axis=1)
                .reshape(512, 128)
                .astype(BF16)
            )

        def block(px):
            lanes = pl.ds(pl.multiple_of(px * 128, 128), 128)
            left = dot(rk[...], dt[:, lanes], 1, 0)
            right = dot(lk[...], dt[lanes, :], 1, 1)
            l_lo, l_hi = swap_halves(left[0:256], left[256:512])
            r_lo, r_hi = swap_halves(right[0:256], right[256:512])
            shape = (16, 2, 8, 128)
            send4[pl.ds(px * 32, 16)] = jnp.concatenate([l_lo.reshape(shape), r_lo.reshape(shape)], axis=2).astype(BF16)
            send4[pl.ds(px * 32 + 16, 16)] = jnp.concatenate(
                [l_hi.reshape(shape), r_hi.reshape(shape)], axis=2
            ).astype(BF16)
            send_x(px, lambda dev, t: remote(send4.at[t], got4.at[chan], P4 + zl, dev).start())

        by_x(block)
        got4[pl.ds(chan, 1)] = send4[pl.ds(me, 1)]

    def outputs(s, carry):
        at = pl.ds(pl.multiple_of(s * 128, 128), 128)
        proj = dot(tri_n[s], wo[...], 0, 0)
        cells(update, s, gate[s] * proj)
        dg = (slope[s] * proj).astype(BF16)
        d_gate[at, :] = dg
        dn[s] = dot(dg, wog[...], 1, 1)
        part[512:640, :] += dot(tri_n[s], d_out[at, :], 1, 0)
        part[640:768, :] += dot(normed[s], dg, 0, 0)
        return carry

    part[512:768, :] = jnp.zeros((256, 128), F32)
    lax.fori_loop(0, 8, outputs, 0)
    stores[0].start()
    for i in range(2):
        out_norms[i : i + 1, :] = jnp.sum(acc[i].T, axis=0, keepdims=True)

    x4 = []
    for half in range(2):
        wait_half(got4, half, rsem.at[(P4, P4B)[half]])
        part4 = pl.ds(half * 32, 32)
        x4.append(remote(got4.at[part4, 1 - q], take4.at[part4], (X4, X4B)[half], sibling))
        x4[half].start()
        ours = pl.ds(pl.multiple_of(q * 1024 + half * 512, 512), 512)
        stage[ours, :] = got4[part4, pl.ds(q, 1)].astype(F32).reshape(512, 128)
    def sides(core):
        def step(s, carry):
            m = mask[pl.ds(s, 1), :]
            rows = pl.ds(pl.multiple_of(core * 64, 64), 64)
            for side in range(2):
                d = stage[pl.ds(core * 1024 + side * 8 + s, 64, stride=16), :] * m
                val, sig = vs[side * 2, s, rows, :], vs[side * 2 + 1, s, rows, :]
                start = pl.multiple_of(side * 256 + core * 64, 64)
                dx[s, pl.ds(start, 64), :] = (d * sig).astype(BF16)
                dx[s, pl.ds(start + 128, 64), :] = (d * val * sig * (1.0 - sig)).astype(BF16)
            return carry

        lax.fori_loop(0, 8, step, 0)

    sides(q)
    for half in range(2):
        x4[half].wait()
        theirs = pl.ds(pl.multiple_of((1 - q) * 1024 + half * 512, 512), 512)
        stage[theirs, :] = take4[half * 32 : half * 32 + 32].astype(F32).reshape(512, 128)
    sides(1 - q)

    def inward(s, carry):
        g = dx[s]
        total = dn[s] + dot(g, wcat[...], 0, 1)
        dn[s] = total
        acc[2] += total * hat_in[s]
        acc[3] += total
        part[0:512, :] += dot(g, normed[s], 1, 0)
        return carry

    part[0:512, :] = jnp.zeros((512, 128), F32)
    lax.fori_loop(0, 8, inward, 0)
    norms = jnp.concatenate(
        [
            jnp.sum(acc[2], axis=0, keepdims=True),
            jnp.sum(acc[3], axis=0, keepdims=True),
            out_norms[...],
            jnp.zeros((4, 128), F32),
        ],
        axis=0,
    )

    for which in range(2):
        a2_send[which * 16 : which * 16 + 16] = jnp.concatenate(
            [
                part[which * 256 : which * 256 + 256, :].reshape(16, 16, 128),
                part[512 + which * 128 : 640 + which * 128, :].reshape(16, 8, 128),
                jnp.broadcast_to(norms.reshape(1, 8, 128), (16, 8, 128)),
            ],
            axis=1,
        ).astype(BF16)
    slot = q * 16 + plane

    def plane_both(fn):
        each_plane(lambda dev, i: [fn((dev[0], dev[1] // 2 * 2 + core), core * 16 + i) for core in range(2)])
        fn(sibling, (1 - q) * 16 + plane)

    plane_both(lambda dev, i: remote(a2_send.at[i], a2_got.at[slot], A2, dev).start())
    a2_got[pl.ds(slot, 1)] = a2_send[pl.ds(slot, 1)]

    def last(s, carry):
        dhat = dn[s] * in_gain[...]
        hat = hat_in[s]
        mean_d = jnp.mean(dhat, axis=-1, keepdims=True)
        mean_dh = jnp.mean(dhat * hat, axis=-1, keepdims=True)
        cells(grad_pair, s, rstd_in[s] * (dhat - mean_d - hat * mean_dh))
        return carry

    lax.fori_loop(0, 4, last, 0)
    wait_slots(a2_got, 31, rsem.at[A2])
    a3_send[...] = jnp.sum(a2_got[...].astype(F32), axis=0).astype(BF16)
    each_z(lambda dev, i: remote(a3_send, a3_got.at[z], A3, dev).start())
    a3_got[pl.ds(z, 1)] = a3_send[...].reshape(1, 32, 128)
    lax.fori_loop(4, 8, last, 0)
    stores[1].start()
    wait_slots(a3_got, 7, rsem.at[A3])
    total = jnp.sum(a3_got[...].astype(F32), axis=0) * (1.0 / 512.0)
    g_norms[...] = total[24:32]
    a4_send[...] = total.astype(BF16)
    plane_both(lambda dev, i: remote(a4_send, pieces_out.at[slot], A4, dev).start())
    stores[2].start()
    stores[3].start()
    wait_slots(pieces_out, 31, rsem.at[A4])

    wait_owners(send1, ssem.at[P1])
    wait_owners(send3, ssem.at[P3])

    @pl.when(own)
    def _():
        wait_slots(send2, 127, ssem.at[P2 + zl])
        wait_slots(send4, 127, ssem.at[P4 + zl])

    wait_slots(a2_send, 31, ssem.at[A2])
    wait_slots(a3_got, 7, ssem.at[A3])
    wait_slots(pieces_out, 31, ssem.at[A4])
    for store in stores:
        store.wait()


def hand_out(update, grad_pair, pieces, g_norms, *refs):
    outs, held, weights, in_sems, sems = refs[:9], refs[9:13], refs[13], refs[14], refs[15]
    loads = [
        pltpu.make_async_copy(a, b, in_sems.at[i])
        for i, (a, b) in enumerate(zip((pieces, update, grad_pair, g_norms), held))
    ]
    sources = [held[1], held[2]] + [weights.at[i] for i in range(6)] + [held[3].at[pl.ds(0, 4)]]
    copies = [pltpu.make_async_copy(a, b, sems.at[i]) for i, (a, b) in enumerate(zip(sources, outs))]
    for load in loads:
        load.start()
    loads[0].wait()
    for which in range(2):
        piece = held[0][which * 16 : which * 16 + 16].astype(F32)
        both = piece[:, 0:16].reshape(256, 128)
        weights[which * 2] = both[0:128].T
        weights[which * 2 + 1] = both[128:256].T
        weights[4 + which] = piece[:, 16:24].reshape(128, 128)
        for i in (which * 2, which * 2 + 1, 4 + which):
            copies[2 + i].start()
    for load, copy in zip(loads[1:], (copies[0], copies[1], copies[8])):
        load.wait()
        copy.start()
    for copy in copies:
        copy.wait()


def scratch():
    def v(shape, kind=F32):
        return pltpu.VMEM(shape, kind)

    return [
        v((1024, 128)), v((1024, 128)), v((8, 128)),
        v((1024, 128)), v((1024, 128)), v((16, 64), jnp.int32), v((1, 128)), v((1, 128)),
        v((128, 128), BF16), v((128, 128), BF16), v((128, 128), BF16), v((128, 128), BF16),
        v((1, 128)), v((1, 128)), v((128, 128), BF16), v((128, 128), BF16), v((8, 128)),
        v((128, 512), BF16), v((512, 128), BF16),
        v((8, 128, 128)), v((8, 128, 1)), v((8, 128, 128), BF16),
        v((4, 8, 128, 128)), v((2048, 128)),
        v((8, 128, 128)), v((8, 128, 128)), v((1024, 128), BF16),
        v((8, 128, 128)), v((8, 128, 128), BF16), v((1024, 128)),
        v((1024, 128), BF16), v((8, 128, 128)), v((8, 512, 128), BF16),
        v((2, 128, 128)), v((4, 128, 128)),
        v((64, 16, 128), BF16), v((64, 2, 16, 128), BF16), v((128, 2, 16, 128), BF16),
        v((512, 512), BF16), v((512, 512), BF16), v((512, 512), BF16),
        v((128, 16, 128), BF16), v((64, 16, 128), BF16),
        v((32, 16, 128), BF16), v((32, 16, 128), BF16),
        v((32, 16, 128), BF16), v((32, 16, 128), BF16),
        v((64, 16, 128), BF16), v((128, 16, 128), BF16),
        v((512, 512), BF16),
        v((128, 2, 16, 128), BF16), v((64, 2, 16, 128), BF16), v((64, 16, 128), BF16),
        v((768, 128)),
        v((32, 32, 128), BF16), v((32, 32, 128), BF16),
        v((32, 128), BF16), v((8, 32, 128), BF16),
        v((32, 128), BF16), v((2, 128)),
        pltpu.SemaphoreType.DMA((13,)),
        pltpu.SemaphoreType.DMA((4,)),
        pltpu.SemaphoreType.DMA((17,)),
        pltpu.SemaphoreType.DMA((17,)),
        pltpu.SemaphoreType.REGULAR,
    ]


def per_device(
    pair, pair_mask, cotangent, in_gain, in_bias, left_weight, left_gate_weight, right_weight, right_gate_weight,
    out_gain, out_bias, output_weight, output_gate_weight,
):
    hbm = pl.BlockSpec(memory_space=pl.ANY)
    square = jax.ShapeDtypeStruct((128, 128), F32)
    cells = jax.ShapeDtypeStruct((1024, 128), F32)
    found = pl.pallas_call(
        kernel,
        out_shape=(cells, cells, jax.ShapeDtypeStruct((32, 32, 128), BF16), jax.ShapeDtypeStruct((8, 128), F32)),
        in_specs=[hbm] * 13,
        out_specs=(hbm,) * 4,
        scratch_shapes=scratch(),
        name="triangle",
        compiler_params=pltpu.CompilerParams(
            collective_id=1, has_side_effects=True, vmem_limit_bytes=60 * 1024 * 1024
        ),
    )(
        pair.reshape(1024, 128), cotangent.reshape(1024, 128), pair_mask.T, in_gain.reshape(1, 128), in_bias.reshape(1, 128),
        left_weight, left_gate_weight, right_weight, right_gate_weight,
        out_gain.reshape(1, 128), out_bias.reshape(1, 128), output_weight, output_gate_weight,
    )
    outs = pl.pallas_call(
        hand_out,
        out_shape=(cells, cells) + (square,) * 6 + (jax.ShapeDtypeStruct((4, 128), F32),),
        in_specs=[hbm] * 4,
        out_specs=(hbm,) * 9,
        scratch_shapes=[
            pltpu.VMEM((32, 32, 128), BF16),
            pltpu.VMEM((1024, 128), F32),
            pltpu.VMEM((1024, 128), F32),
            pltpu.VMEM((8, 128), F32),
            pltpu.VMEM((6, 128, 128), F32),
            pltpu.SemaphoreType.DMA((4,)),
            pltpu.SemaphoreType.DMA((9,)),
        ],
        name="hand_out",
        compiler_params=pltpu.CompilerParams(vmem_limit_bytes=60 * 1024 * 1024),
    )(*found)
    return (outs[0].reshape(64, 16, 128), outs[1].reshape(64, 16, 128)) + tuple(outs[2:])


def solution(mesh):
    cell, copied = P("row", "col", None), P()
    return jax.shard_map(
        per_device,
        mesh=mesh,
        in_specs=(cell, P("row", "col"), cell) + (copied,) * 10,
        out_specs=(cell, cell) + (copied,) * 7,
        check_vma=False,
    )
```
